256 devices in a mesh: ctx: 16 (over x, y_lo, core), head: 16 (over y_hi, z).
Axes of the slice: x: 4, y: 4 (y_hi: 2, y_lo: 2; y = y_hi * 2 + y_lo), z: 8, core: 2. Of those that a mesh axis runs over, the one named last changes fastest.
Arguments:
- queries: bfloat16 [5120, 7168], P('ctx', 'head'), may hold values from -40 to 40
- keys: bfloat16 [5120, 7168], P('ctx', 'head'), may hold values from -6.1 to 6.1
- values: bfloat16 [5120, 7168], P('ctx', 'head'), may hold values from -6 to 6
- out_fwd: bfloat16 [5120, 7168], P('ctx', 'head'), may hold values from -6 to 6
- d_out: bfloat16 [5120, 7168], P(('ctx', 'head')), may hold values from -6 to 6
- plan: int32 [32], replicated, may hold values from 0 to 31, as said below
Outputs:
- d_queries: bfloat16 [5120, 7168], P('ctx', 'head')
- d_keys: bfloat16 [5120, 7168], P('ctx', 'head')
- d_values: bfloat16 [5120, 7168], P('ctx', 'head')
The draws below stay inside these ranges and needn't reach their ends.
Inputs may be any that keep to these rules, and one draw needn't show every extreme that they name: `plan`: a permutation of 0 to 31.
All inputs are finite; a program needn't handle non-finite values.
Results may differ from the reference program's by a relative error of at most 0.009.
Values may be sent and summed in bfloat16 or wider, within the bound.
No kernel may reach another device: no remote copies, remote signals or barrier semaphores. Data moves between devices by JAX's collectives and lax.ppermute only.
A program may use at most 128 MiB of HBM per device.

```python
import math
import jax
import jax.numpy as jnp
from jax import lax

HD = 112
HEAD_DEV = 4
TOK_DEV = 320
D = 7168
TOKENS = 5120
N_CTX = 16
N_HEAD = 16


def block_order(key):
    count = 2 * (TOKENS // TOK_DEV)
    return jax.random.permutation(jax.random.fold_in(key, 101), count).astype(jnp.int32)


def layout(key):
    half = TOK_DEV // 2
    order = block_order(key)
    rows = jnp.arange(TOKENS, dtype=jnp.int32)
    return order[rows // half] * half + rows % half


def column_slopes():
    heads = D // HD
    index = jnp.arange(D, dtype=jnp.int32) // HD
    return jnp.exp2(-8.0 * (index + 1).astype(jnp.float32) / heads)


def first_column():
    return jnp.arange(D, dtype=jnp.int32) % HD == 0


def draw_plan(key, part):
    return block_order(key)


def draw_keys(key, part):
    pos = layout(key)
    key = jax.random.fold_in(key, 11)
    drawn = jnp.clip(jax.random.normal(key, (TOKENS, D), jnp.float32), -6.0, 6.0)
    ramp = 6.0 * (1.0 - 2.0 * pos.astype(jnp.float32) / (TOKENS - 1))
    result = jnp.where(first_column()[None, :], ramp[:, None], drawn)
    return result.astype(jnp.bfloat16)


def draw_queries(key, part):
    key = jax.random.fold_in(key, 7)
    noise_key, factor_key = jax.random.split(key)
    drawn = jnp.clip(0.5 * jax.random.normal(noise_key, (TOKENS, D), jnp.float32), -3.0, 3.0)
    level = jnp.minimum(24.0, 0.75 * column_slopes() * (TOKENS - 1) * math.sqrt(HD) / 12.0)
    factor = jax.random.uniform(factor_key, (TOKENS, 1), jnp.float32, 0.75, 1.25)
    result = jnp.where(first_column()[None, :], level[None, :] * factor, drawn)
    return result.astype(jnp.bfloat16)


def block_levels(stream_key, shape, pieces, least, largest):
    level = 1.0
    for position, blocks in pieces:
        steps = jax.random.uniform(jax.random.fold_in(jax.random.fold_in(stream_key, 6), position), (blocks,), jnp.float32, least / len(pieces), largest / len(pieces))
        level = level * jnp.repeat(jnp.exp(steps), shape[position] // blocks).reshape((-1,) + (1,) * (len(shape) - 1 - position))
    return level


def gaussian(stream_key, extent, width, limit, shards=(), kind=jnp.bfloat16):
    array = width * jax.random.normal(stream_key, extent, jnp.float32)
    if shards:
        array = array * block_levels(stream_key, extent, shards, -0.22, 0.18)
    return jnp.clip(array, -limit, limit).astype(kind)


def setup_inputs(seed: int = 0) -> dict:
    arg_keys = jax.random.split(jax.random.key(seed), 7)
    return {
        "queries": draw_queries(jax.random.fold_in(arg_keys[6], 71), 0),
        "keys": draw_keys(jax.random.fold_in(arg_keys[6], 71), 0),
        "values": gaussian(arg_keys[2], (TOKENS, D), 1.0, 6.0, ((0, 16), (1, 16))),
        "out_fwd": gaussian(arg_keys[3], (TOKENS, D), 1.0, 6.0, ((0, 16), (1, 16))),
        "d_out": gaussian(arg_keys[4], (TOKENS, D), 1.0, 6.0, ((0, 256),)),
        "plan": draw_plan(jax.random.fold_in(arg_keys[6], 71), 0),
    }


def positions(plan, block):
    starts = plan.astype(jnp.int32) * block
    return (starts[:, None] + jnp.arange(block, dtype=jnp.int32)[None, :]).reshape(-1)

def reference(queries, keys, values, out_fwd, d_out, plan):
    seq = queries.shape[0]
    block = seq // (2 * N_CTX)
    pos = positions(plan, block)
    heads = HEAD_DEV * N_HEAD
    scale = 1.0 / math.sqrt(HD)
    dist = (pos[:, None] - pos[None, :]).astype(jnp.float32)
    visible = pos[:, None] >= pos[None, :]

    def one_head(index):
        slope = jnp.exp2(-8.0 * (index + 1).astype(jnp.float32) / heads)
        start = (index * HD).astype(jnp.int32)
        query = lax.dynamic_slice_in_dim(queries, start, HD, 1)
        key_rows = lax.dynamic_slice_in_dim(keys, start, HD, 1)
        value = lax.dynamic_slice_in_dim(values, start, HD, 1)
        output = lax.dynamic_slice_in_dim(out_fwd, start, HD, 1)
        grad = lax.dynamic_slice_in_dim(d_out, start, HD, 1)
        score = jnp.dot(query, key_rows.T, preferred_element_type=jnp.float32) * scale - slope * dist
        score = jnp.where(visible, score, -1e+30)
        top = lax.optimization_barrier(jnp.max(score, axis=1, keepdims=True))
        total = lax.optimization_barrier(jnp.sum(jnp.where(visible, jnp.exp(score - top), 0.0), axis=1, keepdims=True))
        lse = top + jnp.log(total)
        prob = jnp.where(visible, jnp.exp(score - lse), 0.0)
        delta = lax.optimization_barrier(jnp.sum(grad.astype(jnp.float32) * output.astype(jnp.float32), axis=1, keepdims=True))
        d_value = jnp.dot(prob.astype(jnp.bfloat16).T, grad, preferred_element_type=jnp.float32)
        d_prob = jnp.dot(grad, value.T, preferred_element_type=jnp.float32)
        d_score = (prob * (d_prob - delta)).astype(jnp.bfloat16)
        d_query = jnp.dot(d_score, key_rows, preferred_element_type=jnp.float32) * scale
        d_key = jnp.dot(d_score.T, query, preferred_element_type=jnp.float32) * scale
        return (d_query.astype(jnp.bfloat16), d_key.astype(jnp.bfloat16), d_value.astype(jnp.bfloat16))
    d_query, d_key, d_value = lax.map(one_head, jnp.arange(heads, dtype=jnp.int32))

    def arrange(stack):
        return jnp.transpose(stack, (1, 0, 2)).reshape(seq, heads * HD)
    return (arrange(d_query), arrange(d_key), arrange(d_value))
```

```python
import functools
import math

import jax
import jax.numpy as jnp
from jax import lax
from jax.experimental import pallas as pl
from jax.experimental.pallas import tpu as pltpu
from jax.sharding import Mesh, PartitionSpec as P

HD = 112
W = 128
NX = 4
BLK = 160
OWN = 2 * BLK
QT = 256
QROWS = NX * OWN
NQT = QROWS // QT
HALF = 16 * BLK
KC = 256
SCALE = 1.0 / math.sqrt(HD)
LOG2E = math.log2(math.e)
CEXP = SCALE * LOG2E
NEG = -1e30
LIMIT = 56 * 1024 * 1024
F32 = jnp.float32
BF16 = jnp.bfloat16

VM = pl.BlockSpec(memory_space=pltpu.VMEM)
SM = pl.BlockSpec(memory_space=pltpu.SMEM)


def call(kernel, outs, scratch, name):
    def run(*args):
        specs = [SM if a.dtype == jnp.int32 or a.size <= 8 else VM for a in args]
        return pl.pallas_call(
            kernel,
            out_shape=[jax.ShapeDtypeStruct(s, d) for s, d in outs],
            in_specs=specs,
            out_specs=[VM] * len(outs),
            scratch_shapes=scratch,
            compiler_params=pltpu.CompilerParams(vmem_limit_bytes=LIMIT),
            name=name,
        )(*args)

    return run


def ctx_of(ids, s, dyl, dc):
    x = lax.rem(ids[0] + (NX - s), NX)
    yl = ids[1] if dyl == 0 else 1 - ids[1]
    c = ids[2] if dc == 0 else 1 - ids[2]
    return x * 4 + yl * 2 + c


def cotangent_pack_kernel(d_ref, out_ref):
    out_ref[:, :, HD:] = jnp.zeros((64, 20, W - HD), BF16)
    for n in range(64):
        out_ref[(n % NX) * 16 + n // NX, :, :HD] = d_ref[:, n * HD : (n + 1) * HD]


def pack_kernel(ids, tables, q_ref, k_ref, v_ref, o_ref, *rest):
    kv = rest[0:4]
    qo = rest[4:8]
    skv, sqo = rest[8], rest[9]
    ctx = ctx_of(ids, 0, 0, 0)
    row = lax.broadcasted_iota(jnp.int32, (OWN, W - HD), 0)
    lane = lax.broadcasted_iota(jnp.int32, (OWN, W - HD), 1)
    first, second = tables[3, 2 * ctx] * BLK, tables[3, 2 * ctx + 1] * BLK
    pos = jnp.where(row < BLK, first + row, second + row - BLK)
    high = (pos // 64) * 64
    low = pos - high
    one = jnp.where(lane < 9, 1, 0)
    kx = jnp.where(lane < 3, high, jnp.where(lane < 6, low, one)).astype(F32).astype(BF16)
    vx = jnp.where(lane < 3, 1.0, 0.0).astype(BF16)
    zx = jnp.zeros((OWN, W - HD), BF16)
    for n in range(NX):
        cols = slice(n * HD, (n + 1) * HD)
        skv[n, :OWN, :HD] = k_ref[:, cols]
        skv[n, :OWN, HD:] = kx
        skv[n, OWN:, :HD] = v_ref[:, cols]
        skv[n, OWN:, HD:] = vx
        sqo[n, :OWN, :HD] = q_ref[:, cols]
        sqo[n, :OWN, HD:] = zx
        sqo[n, OWN:, :HD] = o_ref[:, cols]
        sqo[n, OWN:, HD:] = zx
    for s in range(NX):
        head = lax.rem(ids[0] + s, NX)
        kv[s][...] = skv[head]
        qo[s][...] = sqo[head]


def at(start, size):
    return pl.ds(pl.multiple_of(start, 32), size)


def split3(value):
    a = value.astype(BF16)
    r = value - a.astype(F32)
    b = r.astype(BF16)
    return a, b, (r - b.astype(F32)).astype(BF16)


def sort_keys(ids, tables, pieces, dyl, dst, first):
    for s in range(NX):
        for dc in range(2):
            ctx = ctx_of(ids, s, dyl, dc)
            for h in range(2):
                rank = tables[0, 2 * ctx + h]
                dst[at(rank * BLK, BLK), :] = pieces[s * 2 + dc][
                    first + h * BLK : first + (h + 1) * BLK, :
                ]


def sort_rows(ids, tables, blocks, dst):
    for s in range(NX):
        ctx = ctx_of(ids, s, 0, 0)
        for h in range(2):
            dst[at(tables[1, 2 * ctx + h] * BLK, BLK), :] = blocks(s, h)


def sort_limits(ids, tables, limits):
    for s in range(NX):
        ctx = ctx_of(ids, s, 0, 0)
        for h in range(2):
            r = tables[1, 2 * ctx + h]
            limits[0, r] = tables[0, 2 * ctx + h]
            limits[1, r] = tables[2, 2 * ctx + h]


def tile_limits(limits, i, dyl):
    b0, b1 = (QT * i) // BLK, (QT * i + QT - 1) // BLK
    row = lax.broadcasted_iota(jnp.int32, (1, QT), 1) + QT * i
    lim = jnp.zeros((1, QT), jnp.int32)
    for b in range(b0, b1 + 1):
        inside = jnp.logical_and(row >= b * BLK, row < (b + 1) * BLK)
        if dyl == 0:
            value = limits[0, b] * BLK + (row - b * BLK)
        else:
            value = jnp.broadcast_to(limits[1, b] * BLK - 1, (1, QT))
        lim = jnp.where(inside, value, lim)
    full = lax.div(limits[dyl, b0] * BLK, KC)
    last = limits[dyl, b1] * BLK + (BLK if dyl == 0 else 0)
    return lim, full, lax.div(last + KC - 1, KC)


def stats_kernel(ids, tables, slope, *rest):
    kown, koth = rest[0:8], rest[8:16]
    qo = rest[16:20]
    qs, qt = rest[20:22]
    keys, limits = rest[22:24]
    sort_keys(ids, tables, kown, 0, keys.at[0], 0)
    sort_keys(ids, tables, koth, 1, keys.at[1], 0)
    sort_rows(ids, tables, lambda s, h: qo[s][h * BLK : (h + 1) * BLK, :], qs)
    sort_limits(ids, tables, limits)
    m1, m2, m3 = split3(jnp.full((1, QT), slope[0] / SCALE, F32))
    for i in range(NQT):
        cols = slice(i * QT, (i + 1) * QT)
        qt[:, cols] = qs[cols, :].T
        qt[HD : HD + 16, cols] = jnp.concatenate(
            [m1, m2, m3, m1, m2, m3, jnp.zeros((10, QT), BF16)], axis=0
        )
        qti = qt[:, cols]
        state = (jnp.full((8, QT), NEG, F32), jnp.zeros((8, QT), F32))
        for dyl in range(2):
            lim, full, end = tile_limits(limits, i, dyl)

            def step(j, state, masked, dyl=dyl, lim=lim, qti=qti):
                top, total = state
                s = jnp.dot(keys[dyl, at(j * KC, KC), :], qti, preferred_element_type=F32)
                if masked:
                    index = lax.broadcasted_iota(jnp.int32, (KC, QT), 0) + j * KC
                    s = jnp.where(index <= lim, s, NEG)
                s = s.reshape(KC // 8, 8, QT)
                new = jnp.maximum(top, jnp.max(s, axis=0))
                e = jnp.exp2((s - new[None]) * CEXP)
                total = total * jnp.exp2((top - new) * CEXP) + jnp.sum(e, axis=0)
                return new, total

            state = lax.fori_loop(0, full, functools.partial(step, masked=False), state)
            state = lax.fori_loop(full, end, functools.partial(step, masked=True), state)
        top8, total8 = state
        top = jnp.max(top8, axis=0, keepdims=True)
        total = jnp.sum(total8 * jnp.exp2((top8 - top) * CEXP), axis=0, keepdims=True)
        l1, l2, l3 = split3(-(top + jnp.log(total) * (1.0 / SCALE)))
        qt[HD : HD + 16, cols] = jnp.concatenate(
            [m1, m2, m3, m1, m2, m3, l1, l2, l3, jnp.zeros((7, QT), BF16)], axis=0
        )


def grads_loop(dyl, keys, vals, qs, qt, dos, dot, limits, dkey, dval, dq):
    dkey[...] = jnp.zeros((HALF, W), F32)
    dval[...] = jnp.zeros((HALF, W), F32)
    for i in range(NQT):
        cols = slice(i * QT, (i + 1) * QT)
        lim, full, end = tile_limits(limits, i, dyl)

        def step(j, carry, masked, cols=cols, lim=lim):
            rows = at(j * KC, KC)
            kc = keys[rows, :]
            s = jnp.dot(kc, qt[:, cols], preferred_element_type=F32)
            p = jnp.exp2(s * CEXP)
            if masked:
                index = lax.broadcasted_iota(jnp.int32, (KC, QT), 0) + j * KC
                p = jnp.where(index <= lim, p, 0.0)
            dp = jnp.dot(vals[rows, :], dot[:, cols], preferred_element_type=F32)
            ds = (p * dp).astype(BF16)
            dval[rows, :] += jnp.dot(p.astype(BF16), dos[cols, :], preferred_element_type=F32)
            dkey[rows, :] += jnp.dot(ds, qs[cols, :], preferred_element_type=F32)
            dq[cols, :] += lax.dot_general(
                ds, kc, (((0,), (0,)), ((), ())), preferred_element_type=F32
            )
            return carry

        lax.fori_loop(0, full, functools.partial(step, masked=False), 0)
        lax.fori_loop(full, end, functools.partial(step, masked=True), 0)


def unsort(ids, tables, dyl, dc, dkey, dval, out):
    for s in range(NX):
        ctx = ctx_of(ids, s, dyl, dc)
        for h in range(2):
            rows = at(tables[0, 2 * ctx + h] * BLK, BLK)
            base = s * 2 * OWN + h * BLK
            out[base : base + BLK, :] = (dkey[rows, :] * SCALE).astype(BF16)
            out[base + OWN : base + OWN + BLK, :] = dval[rows, :].astype(BF16)


def grads_other_kernel(ids, tables, *rest):
    kv = rest[0:8]
    qo = rest[8:12]
    dor, qs, qt = rest[12:15]
    dos, dot, dq, keep, send = rest[15:20]
    keys, vals, dkey, dval, flat, outs, limits = rest[20:27]
    sort_keys(ids, tables, kv, 1, keys, 0)
    sort_keys(ids, tables, kv, 1, vals, OWN)
    sort_limits(ids, tables, limits)
    for n in range(64):
        flat[n * 20 : (n + 1) * 20, :] = dor[n]

    def block(s, h):
        x = lax.rem(ids[0] + (NX - s), NX)
        return flat[at(x * OWN + h * BLK, BLK), :]

    sort_rows(ids, tables, block, dos)
    sort_rows(ids, tables, lambda s, h: qo[s][OWN + h * BLK : OWN + (h + 1) * BLK, :], outs)
    for i in range(NQT):
        cols = slice(i * QT, (i + 1) * QT)
        prod = dos[cols, :].astype(F32) * outs[cols, :].astype(F32)
        delta = jnp.sum(prod.T, axis=0, keepdims=True)
        d1, d2, d3 = split3(-delta)
        dot[:, cols] = dos[cols, :].T
        dot[HD : HD + 16, cols] = jnp.concatenate(
            [d1, d2, d3, jnp.zeros((13, QT), BF16)], axis=0
        )
    dq[...] = jnp.zeros((QROWS, W), F32)
    grads_loop(1, keys, vals, qs, qt, dos, dot, limits, dkey, dval, dq)
    unsort(ids, tables, 1, 0, dkey, dval, keep)
    unsort(ids, tables, 1, 1, dkey, dval, send)


def grads_own_kernel(ids, tables, *rest):
    kv = rest[0:8]
    qs, qt, dos, dot, dq_in = rest[8:13]
    dqo = rest[13:17]
    keep, send = rest[17:19]
    keys, vals, dkey, dval, dq, limits = rest[19:25]
    sort_keys(ids, tables, kv, 0, keys, 0)
    sort_keys(ids, tables, kv, 0, vals, OWN)
    sort_limits(ids, tables, limits)
    dq[...] = dq_in[...]
    grads_loop(0, keys, vals, qs, qt, dos, dot, limits, dkey, dval, dq)
    unsort(ids, tables, 0, 0, dkey, dval, keep)
    unsort(ids, tables, 0, 1, dkey, dval, send)
    for s in range(NX):
        ctx = ctx_of(ids, s, 0, 0)
        for h in range(2):
            rows = at(tables[1, 2 * ctx + h] * BLK, BLK)
            dqo[s][h * BLK : (h + 1) * BLK, :] = (dq[rows, :] * SCALE).astype(BF16)


def add_kernel(a, b, out):
    out[...] = (a[...].astype(F32) + b[...].astype(F32)).astype(BF16)


def add3_kernel(a, b, c, *outs):
    for s in range(NX):
        rows = slice(s * 2 * OWN, (s + 1) * 2 * OWN)
        outs[s][...] = (
            a[rows, :].astype(F32) + b[rows, :].astype(F32) + c[rows, :].astype(F32)
        ).astype(BF16)


def unpack_kernel(ids, *rest):
    dq, dkv = rest[0:4], rest[4:8]
    oq, ok, ov = rest[8:11]
    sq, skv = rest[11:13]
    for s in range(NX):
        head = lax.rem(ids[0] + s, NX)
        sq[head] = dq[s][...]
        skv[head] = dkv[s][...]
    for n in range(NX):
        cols = slice(n * HD, (n + 1) * HD)
        oq[:, cols] = sq[n, :, :HD]
        ok[:, cols] = skv[n, :OWN, :HD]
        ov[:, cols] = skv[n, OWN:, :HD]


def shift(value, axis, by):
    n = lax.axis_size(axis)
    return lax.ppermute(value, axis, [(i, (i + by) % n) for i in range(n)])


def plan_tables(plan):
    block = jnp.arange(32, dtype=jnp.int32)
    half = (block >> 2) & 1
    group = (block >> 1) & 3
    before = plan[None, :] < plan[:, None]
    same_half = half[None, :] == half[:, None]
    same_group = group[None, :] == group[:, None]

    def count(m):
        return jnp.sum(jnp.where(jnp.logical_and(before, m), 1, 0), axis=1, dtype=jnp.int32)

    return jnp.stack([count(same_half), count(same_group), count(jnp.logical_not(same_half)), plan])


def on_device(queries, keys, values, out_fwd, d_out, plan):
    piece = ((2 * OWN, W), BF16)
    stack = ((NX * 2 * OWN, W), BF16)
    x = lax.axis_index("x")
    ids = jnp.stack([x, lax.axis_index("yl"), lax.axis_index("c")]).astype(jnp.int32)
    tables = plan_tables(plan)
    head_id = (lax.axis_index("yh") * 8 + lax.axis_index("z")) * NX + x
    slope = jnp.exp2(-8.0 * (head_id + 1).astype(F32) / 64.0).reshape(1)

    (d_pack,) = call(cotangent_pack_kernel, [((64, 20, W), BF16)], [], "cotangent_pack")(d_out)
    d_rows = lax.all_to_all(d_pack, ("x", "yh", "z"), 0, 0)

    packed = call(
        pack_kernel,
        [piece] * 8,
        [pltpu.VMEM((NX, 2 * OWN, W), BF16)] * 2,
        "pack",
    )(ids, tables, queries, keys, values, out_fwd)
    kv, qo = list(packed[:4]), list(packed[4:])
    for s in (1, 3, 2):
        kv[s] = shift(kv[s], "x", s)
    for s in (1, 3, 2):
        qo[s] = shift(qo[s], "x", s)
    kv_y = [shift(a, "yl", 1) for a in kv]
    kv_c = [shift(a, "c", 1) for a in kv]
    kv_yc = [shift(a, "c", 1) for a in kv_y]
    own = [a for s in range(NX) for a in (kv[s], kv_c[s])]
    other = [a for s in range(NX) for a in (kv_y[s], kv_yc[s])]

    limits = pltpu.SMEM((2, 8), jnp.int32)
    qs, qt = call(
        stats_kernel,
        [((QROWS, W), BF16), ((W, QROWS), BF16)],
        [pltpu.VMEM((2, HALF, W), BF16), limits],
        "stats",
    )(ids, tables, slope, *own, *other, *qo)
    accs = [pltpu.VMEM((HALF, W), BF16)] * 2 + [pltpu.VMEM((HALF, W), F32)] * 2
    dos, dot, dq, keep_o, send_o = call(
        grads_other_kernel,
        [((QROWS, W), BF16), ((W, QROWS), BF16), ((QROWS, W), F32), stack, stack],
        accs + [pltpu.VMEM((QROWS, W), BF16)] * 2 + [limits],
        "grads_other",
    )(ids, tables, *other, *qo, d_rows, qs, qt)
    recv_o = shift(send_o, "c", 1)
    (sum_o,) = call(add_kernel, [stack], [], "add_other")(keep_o, recv_o)
    recv_y = shift(sum_o, "yl", 1)

    *dqs, keep, send = call(
        grads_own_kernel,
        [((OWN, W), BF16)] * 4 + [stack, stack],
        accs + [pltpu.VMEM((QROWS, W), F32), limits],
        "grads_own",
    )(ids, tables, *own, qs, qt, dos, dot, dq)
    recv = shift(send, "c", 1)
    dqs = [dqs[0]] + [shift(dqs[s], "x", -s) for s in (1, 2, 3)]
    dkvs = call(add3_kernel, [piece] * 4, [], "add_own")(keep, recv, recv_y)
    dkvs = [dkvs[0]] + [shift(dkvs[s], "x", -s) for s in (1, 2, 3)]
    out = ((OWN, NX * HD), BF16)
    return tuple(
        call(
            unpack_kernel,
            [out] * 3,
            [pltpu.VMEM((NX, OWN, W), BF16), pltpu.VMEM((NX, 2 * OWN, W), BF16)],
            "unpack",
        )(ids, *dqs, *dkvs)
    )


def solution(mesh):
    devices = mesh.devices.reshape(4, 2, 2, 2, 8)
    fine = Mesh(devices, ("x", "yl", "c", "yh", "z"))
    ctx, head = ("x", "yl", "c"), ("yh", "z")
    tile = P(ctx, head)
    return jax.shard_map(
        on_device,
        mesh=fine,
        in_specs=(tile, tile, tile, tile, P(ctx + head, None), P()),
        out_specs=(tile, tile, tile),
        check_vma=False,
    )
```

```python
import functools
import math

import jax
import jax.numpy as jnp
from jax import lax
from jax.experimental import pallas as pl
from jax.experimental.pallas import tpu as pltpu
from jax.sharding import Mesh, PartitionSpec as P

HD = 112
W = 128
NX = 4
BLK = 160
OWN = 2 * BLK
QT = 256
QROWS = NX * OWN
NQT = QROWS // QT
HALF = 16 * BLK
SKC = 512
SPER = 4
GKC = 640
GPER = 2
DROWS = QROWS + QT
SCALE = 1.0 / math.sqrt(HD)
LOG2E = math.log2(math.e)
CEXP = SCALE * LOG2E
NEG = -1e30
LIMIT = 56 * 1024 * 1024
F32 = jnp.float32
BF16 = jnp.bfloat16

VM = pl.BlockSpec(memory_space=pltpu.VMEM)
SM = pl.BlockSpec(memory_space=pltpu.SMEM)


def call(kernel, outs, scratch, name, after=0):
    def run(*args):
        specs = [SM if a.dtype == jnp.int32 or a.size <= 8 else VM for a in args]
        if after:
            specs[-after:] = [pl.BlockSpec(memory_space=pl.ANY)] * after
        return pl.pallas_call(
            kernel,
            out_shape=[jax.ShapeDtypeStruct(s, d) for s, d in outs],
            in_specs=specs,
            out_specs=[VM] * len(outs),
            scratch_shapes=scratch,
            compiler_params=pltpu.CompilerParams(vmem_limit_bytes=LIMIT),
            name=name,
        )(*args)

    return run


def ctx_of(ids, s, dyl, dc):
    x = lax.rem(ids[0] + (NX - s), NX)
    yl = ids[1] if dyl == 0 else 1 - ids[1]
    c = ids[2] if dc == 0 else 1 - ids[2]
    return x * 4 + yl * 2 + c


def cotangent_pack_kernel(d_ref, out_ref):
    out_ref[:, :, HD:] = jnp.zeros((64, 20, W - HD), BF16)
    for n in range(64):
        out_ref[(n % NX) * 16 + n // NX, :, :HD] = d_ref[:, n * HD : (n + 1) * HD]


def here():
    return lax.axis_index("x"), lax.axis_index("yl"), lax.axis_index("c")


def key_columns(plan):
    ctx = ctx_of(here(), 0, 0, 0)
    row = lax.broadcasted_iota(jnp.int32, (OWN, W - HD), 0)
    lane = lax.broadcasted_iota(jnp.int32, (OWN, W - HD), 1)
    first, second = plan[2 * ctx] * BLK, plan[2 * ctx + 1] * BLK
    pos = jnp.where(row < BLK, first + row, second + row - BLK)
    high = (pos // 64) * 64
    one = jnp.where(lane < 9, 1, 0)
    return jnp.where(lane < 3, high, jnp.where(lane < 6, pos - high, one)).astype(F32).astype(BF16)


def pack_kernel(extras, plan, a_ref, b_ref, *rest):
    outs, buf = rest[-5:-1], rest[-1]
    if extras == "kv":
        lane = lax.broadcasted_iota(jnp.int32, (OWN, W - HD), 1)
        wide = (key_columns(plan), jnp.where(lane < 3, 1.0, 0.0).astype(BF16))
    else:
        wide = (jnp.zeros((OWN, W - HD), BF16),) * 2
    for n in range(NX):
        for i, ref in enumerate((a_ref, b_ref)):
            rows = slice(i * OWN, (i + 1) * OWN)
            buf[n, rows, :HD] = ref[:, n * HD : (n + 1) * HD]
            buf[n, rows, HD:] = wide[i]
    x = lax.axis_index("x")
    for s in range(NX):
        outs[s][...] = buf[lax.rem(x + s, NX)]


def at(start, size):
    return pl.ds(pl.multiple_of(start, 32), size)


def split3(value):
    a = value.astype(BF16)
    r = value - a.astype(F32)
    b = r.astype(BF16)
    return a, b, (r - b.astype(F32)).astype(BF16)


def sort_keys(ids, tables, row, dyl, pieces, first, swapped, second, dst):
    for s in range(NX):
        for dc in range(2):
            ctx = ctx_of(ids, s, dyl, dc)
            for h in range(2):
                src, base = (pieces[s], first) if dc == 0 else (swapped, 2 * s * OWN + second)
                base = base + h * BLK
                dst[at(tables[row, 2 * ctx + h] * BLK, BLK), :] = src[base : base + BLK, :]


def sort_rows(ids, tables, blocks, dst):
    for s in range(NX):
        ctx = ctx_of(ids, s, 0, 0)
        for h in range(2):
            dst[at(tables[1, 2 * ctx + h] * BLK, BLK), :] = blocks(s, h)


def sort_limits(ids, tables, limits):
    for s in range(NX):
        ctx = ctx_of(ids, s, 0, 0)
        for h in range(2):
            r = tables[1, 2 * ctx + h]
            limits[0, r] = tables[0, 2 * ctx + h]
            limits[1, r] = tables[2, 2 * ctx + h]
            limits[2, r] = tables[3, 2 * ctx + h]


def tile_limits(limits, i, dyl):
    b0, b1 = (QT * i) // BLK, (QT * i + QT - 1) // BLK
    row = lax.broadcasted_iota(jnp.int32, (1, QT), 1) + QT * i
    lim = jnp.zeros((1, QT), jnp.int32)
    for b in range(b0, b1 + 1):
        inside = jnp.logical_and(row >= b * BLK, row < (b + 1) * BLK)
        if dyl == 1:
            value = jnp.broadcast_to(limits[1, b] * BLK - 1, (1, QT))
        else:
            value = limits[dyl, b] * BLK + (row - b * BLK)
        lim = jnp.where(inside, value, lim)
    return lim, limits[dyl, b1] * BLK + (0 if dyl == 1 else BLK)


def list_work(limits, dyl, size, per, work, lims):
    count = jnp.int32(0)
    for i in range(NQT):
        lim, last = tile_limits(limits, i, dyl)
        lims[i] = lim
        n = lax.div(last + size - 1, size)

        def put(k, carry, i=i, count=count):
            work[0, count + k] = i
            work[1, count + k] = k
            return carry

        lax.fori_loop(0, n, put, 0)
        count = count + n
    lims[NQT] = jnp.full((1, QT), -1, jnp.int32)
    for u in range(per - 1):
        work[0, count + u] = NQT
        work[1, count + u] = 0
    return lax.div(count + per - 1, per)


def stats_kernel(tables, slope, *rest):
    ids = here()
    qo, kv, kv_y, kv_c, kv_yc = rest[0:4], rest[4:8], rest[8:12], rest[12], rest[13]
    qs, qt = rest[14:16]
    keys, limits, work, lims, tops, totals = rest[16:22]
    sort_keys(ids, tables, 3, 0, kv, 0, kv_c, 0, keys)
    sort_keys(ids, tables, 3, 1, kv_y, 0, kv_yc, 0, keys)
    sort_rows(ids, tables, lambda s, h: qo[s][h * BLK : (h + 1) * BLK, :], qs)
    qs[QROWS:, :] = jnp.zeros((QT, W), BF16)
    sort_limits(ids, tables, limits)
    m1, m2, m3 = split3(jnp.full((1, QT), slope[0] / SCALE, F32))
    for i in range(NQT):
        qt[i] = qs[i * QT : (i + 1) * QT, :].T
        qt[i, HD : HD + 16, :] = jnp.concatenate(
            [m1, m2, m3, m1, m2, m3, jnp.zeros((10, QT), BF16)], axis=0
        )
    qt[NQT] = jnp.zeros((W, QT), BF16)
    steps = list_work(limits, 2, SKC, SPER, work, lims)
    tops[...] = jnp.full(tops.shape, NEG, F32)
    totals[...] = jnp.zeros(totals.shape, F32)

    def step(j, carry):
        for u in range(SPER):
            item = j * SPER + u
            tile, chunk = work[0, item], work[1, item]
            s = jnp.dot(keys[at(chunk * SKC, SKC), :], qt[tile], preferred_element_type=F32)
            index = lax.broadcasted_iota(jnp.int32, (SKC, QT), 0)
            s = jnp.where(index <= lims[tile] - chunk * SKC, s, NEG)
            s = s.reshape(SKC // 8, 8, QT)
            top = jnp.max(s, axis=0)
            tops[tile, chunk] = top
            totals[tile, chunk] = jnp.sum(jnp.exp2((s - top[None]) * CEXP), axis=0)
        return carry

    lax.fori_loop(0, steps, step, 0)
    for i in range(NQT):
        top = jnp.max(jnp.max(tops[i], axis=0), axis=0, keepdims=True)
        total8 = jnp.sum(totals[i] * jnp.exp2((tops[i] - top) * CEXP), axis=0)
        total = jnp.sum(total8, axis=0, keepdims=True)
        l1, l2, l3 = split3(-(top + jnp.log(total) * (1.0 / SCALE)))
        qt[i, HD : HD + 16, :] = jnp.concatenate(
            [m1, m2, m3, m1, m2, m3, l1, l2, l3, jnp.zeros((7, QT), BF16)], axis=0
        )


def grads_loop(dyl, keys, vals, qs, qt, dos, dot, limits, dkey, dval, dq, work, lims):
    dkey[...] = jnp.zeros((HALF, W), F32)
    dval[...] = jnp.zeros((HALF, W), F32)
    steps = list_work(limits, dyl, GKC, GPER, work, lims)

    def step(j, carry):
        parts = []
        for u in range(GPER):
            item = j * GPER + u
            tile, chunk = work[0, item], work[1, item]
            rows = at(chunk * GKC, GKC)
            cols = at(tile * QT, QT)
            kc = keys[rows, :]
            s = jnp.dot(kc, qt[tile], preferred_element_type=F32)
            index = lax.broadcasted_iota(jnp.int32, (GKC, QT), 0)
            p = jnp.where(index <= lims[tile] - chunk * GKC, jnp.exp2(s * CEXP), 0.0)
            dp = jnp.dot(vals[rows, :], dot[tile], preferred_element_type=F32)
            ds = (p * dp).astype(BF16)
            dv = jnp.dot(p.astype(BF16), dos[cols, :], preferred_element_type=F32)
            dk = jnp.dot(ds, qs[cols, :], preferred_element_type=F32)
            d = lax.dot_general(ds, kc, (((0,), (0,)), ((), ())), preferred_element_type=F32)
            parts.append((rows, cols, dv, dk, d))
        for rows, cols, dv, dk, d in parts:
            dval[rows, :] += dv
            dkey[rows, :] += dk
            dq[cols, :] += d
        return carry

    lax.fori_loop(0, steps, step, 0)


def unsort(ids, tables, dyl, dc, dkey, dval, out):
    for s in range(NX):
        ctx = ctx_of(ids, s, dyl, dc)
        for h in range(2):
            rows = at(tables[0, 2 * ctx + h] * BLK, BLK)
            base = s * 2 * OWN + h * BLK
            out[base : base + BLK, :] = (dkey[rows, :] * SCALE).astype(BF16)
            out[base + OWN : base + OWN + BLK, :] = dval[rows, :].astype(BF16)


def grads_other_kernel(tables, *rest):
    ids = here()
    qo, kv_y, kv_yc = rest[0:4], rest[4:8], rest[8]
    dor, qs, qt = rest[9:12]
    dos, dot, dq, keep, send = rest[12:17]
    keys, vals, dkey, dval, work, lims, flat, outs, limits = rest[17:26]
    sort_keys(ids, tables, 0, 1, kv_y, 0, kv_yc, 0, keys)
    sort_keys(ids, tables, 0, 1, kv_y, OWN, kv_yc, OWN, vals)
    sort_limits(ids, tables, limits)
    for n in range(64):
        flat[n * 20 : (n + 1) * 20, :] = dor[n]

    def block(s, h):
        x = lax.rem(ids[0] + (NX - s), NX)
        return flat[at(x * OWN + h * BLK, BLK), :]

    sort_rows(ids, tables, block, dos)
    sort_rows(ids, tables, lambda s, h: qo[s][OWN + h * BLK : OWN + (h + 1) * BLK, :], outs)
    for i in range(NQT):
        cols = slice(i * QT, (i + 1) * QT)
        prod = dos[cols, :].astype(F32) * outs[cols, :].astype(F32)
        delta = jnp.sum(prod.T, axis=0, keepdims=True)
        d1, d2, d3 = split3(-delta)
        dot[i] = dos[cols, :].T
        dot[i, HD : HD + 16, :] = jnp.concatenate(
            [d1, d2, d3, jnp.zeros((13, QT), BF16)], axis=0
        )
    dot[NQT] = jnp.zeros((W, QT), BF16)
    dos[QROWS:, :] = jnp.zeros((QT, W), BF16)
    dq[...] = jnp.zeros((DROWS, W), F32)
    grads_loop(1, keys, vals, qs, qt, dos, dot, limits, dkey, dval, dq, work, lims)
    unsort(ids, tables, 1, 0, dkey, dval, keep)
    unsort(ids, tables, 1, 1, dkey, dval, send)


def grads_own_kernel(tables, *rest):
    ids = here()
    kv, kv_c = rest[0:4], rest[4]
    qs, qt, dos, dot, dq_in = rest[5:10]
    dqo, keep, send = rest[10:13]
    keys, vals, dkey, dval, work, lims, dq, limits = rest[13:21]
    sort_keys(ids, tables, 0, 0, kv, 0, kv_c, 0, keys)
    sort_keys(ids, tables, 0, 0, kv, OWN, kv_c, OWN, vals)
    sort_limits(ids, tables, limits)
    dq[...] = dq_in[...]
    grads_loop(0, keys, vals, qs, qt, dos, dot, limits, dkey, dval, dq, work, lims)
    unsort(ids, tables, 0, 0, dkey, dval, keep)
    unsort(ids, tables, 0, 1, dkey, dval, send)
    for s in range(NX):
        ctx = ctx_of(ids, s, 0, 0)
        for h in range(2):
            rows = at(tables[1, 2 * ctx + h] * BLK, BLK)
            base = s * OWN + h * BLK
            dqo[base : base + BLK, :] = (dq[rows, :] * SCALE).astype(BF16)


def add_kernel(a, b, out):
    out[...] = (a[...].astype(F32) + b[...].astype(F32)).astype(BF16)


def add_own_kernel(a, b, c, dq, *outs):
    for s in range(NX):
        rows = slice(s * 2 * OWN, (s + 1) * 2 * OWN)
        outs[s][:OWN, :] = dq[s * OWN : (s + 1) * OWN, :]
        total = a[rows, :].astype(F32) + b[rows, :].astype(F32) + c[rows, :].astype(F32)
        outs[s][OWN:, :] = total.astype(BF16)


def unpack_kernel(*rest):
    pieces, outs, buf = rest[0:4], rest[4:7], rest[7]
    x = lax.axis_index("x")
    for s in range(NX):
        buf[lax.rem(x + s, NX)] = pieces[s][...]
    for n in range(NX):
        for i in range(3):
            outs[i][:, n * HD : (n + 1) * HD] = buf[n, i * OWN : (i + 1) * OWN, :HD]


def shift(value, by, flip=False):
    pairs = []
    for x in range(NX):
        for yl in range(2):
            pairs.append((2 * x + yl, 2 * ((x + by) % NX) + (1 - yl if flip else yl)))
    return lax.ppermute(value, ("x", "yl"), pairs)


def swap_core(value):
    return lax.ppermute(value, "c", [(0, 1), (1, 0)])


def worklist(size, keys, per):
    items = NQT * (keys // size) + per
    return [pltpu.SMEM((2, items), jnp.int32), pltpu.VMEM((NQT + 1, 1, QT), jnp.int32)]


def plan_tables(plan):
    block = jnp.arange(32, dtype=jnp.int32)
    half = (block >> 2) & 1
    group = (block >> 1) & 3
    before = plan[None, :] < plan[:, None]
    same_half = half[None, :] == half[:, None]
    same_group = group[None, :] == group[:, None]

    def count(m):
        return jnp.sum(jnp.where(jnp.logical_and(before, m), 1, 0), axis=1, dtype=jnp.int32)

    return jnp.stack([count(same_half), count(same_group), count(jnp.logical_not(same_half)), plan])


def on_device(queries, keys, values, out_fwd, d_out, plan):
    piece = ((2 * OWN, W), BF16)
    stack = ((NX * 2 * OWN, W), BF16)
    x = lax.axis_index("x")
    tables = plan_tables(plan)
    head_id = (lax.axis_index("yh") * 8 + lax.axis_index("z")) * NX + x
    slope = jnp.exp2(-8.0 * (head_id + 1).astype(F32) / 64.0).reshape(1)

    buf = [pltpu.VMEM((NX, 2 * OWN, W), BF16)]
    kv = call(functools.partial(pack_kernel, "kv"), [piece] * 4, buf, "pack_kv")(plan, keys, values)
    kv, d_out = lax.optimization_barrier((kv, d_out))
    (d_pack,) = call(cotangent_pack_kernel, [((64, 20, W), BF16)], [], "cotangent_pack")(d_out)
    d_rows = lax.all_to_all(d_pack, ("x", "yh", "z"), 0, 0)
    kv = [kv[0]] + [shift(kv[s], s) for s in (1, 2, 3)]
    qo = call(functools.partial(pack_kernel, "qo"), [piece] * 4, buf, "pack_qo", 4)(
        plan, queries, out_fwd, *kv[1:], tables
    )
    kv_y = [shift(a, 0, True) for a in kv]
    qo = [qo[0]] + [shift(qo[s], s) for s in (1, 2, 3)]
    kv_y, qo, d_rows = lax.optimization_barrier((kv_y, qo, d_rows))
    kv_c = swap_core(jnp.concatenate(kv))
    kv_yc = swap_core(jnp.concatenate(kv_y))

    limits = pltpu.SMEM((3, 8), jnp.int32)
    qs, qt = call(
        stats_kernel,
        [((DROWS, W), BF16), ((NQT + 1, W, QT), BF16)],
        [pltpu.VMEM((2 * HALF, W), BF16), limits]
        + worklist(SKC, 2 * HALF, SPER)
        + [pltpu.VMEM((NQT + 1, 2 * HALF // SKC, 8, QT), F32)] * 2,
        "stats",
    )(tables, slope, *qo, *kv, *kv_y, kv_c, kv_yc)
    accs = [pltpu.VMEM((HALF, W), BF16)] * 2 + [pltpu.VMEM((HALF, W), F32)] * 2
    accs = accs + worklist(GKC, HALF, GPER)
    dos, dot, dq, keep, send = call(
        grads_other_kernel,
        [((DROWS, W), BF16), ((NQT + 1, W, QT), BF16), ((DROWS, W), F32), stack, stack],
        accs + [pltpu.VMEM((QROWS, W), BF16)] * 2 + [limits],
        "grads_other",
    )(tables, *qo, *kv_y, kv_yc, d_rows, qs, qt)
    (dkv_y,) = call(add_kernel, [stack], [], "add_other")(keep, swap_core(send))
    dq, dkv_y = lax.optimization_barrier((dq, dkv_y))
    dkv_y = shift(dkv_y, 0, True)

    dq, keep, send = call(
        grads_own_kernel,
        [((QROWS, W), BF16), stack, stack],
        accs + [pltpu.VMEM((DROWS, W), F32), limits],
        "grads_own",
    )(tables, *kv, kv_c, qs, qt, dos, dot, dq)
    send, dkv_y = lax.optimization_barrier((send, dkv_y))
    grads = call(add_own_kernel, [((3 * OWN, W), BF16)] * 4, [], "add_own")(
        keep, swap_core(send), dkv_y, dq
    )
    grads = [grads[0]] + [shift(grads[s], -s) for s in (1, 2, 3)]
    return tuple(
        call(
            unpack_kernel,
            [((OWN, NX * HD), BF16)] * 3,
            [pltpu.VMEM((NX, 3 * OWN, W), BF16)],
            "unpack",
        )(*grads)
    )


def solution(mesh):
    devices = mesh.devices.reshape(4, 2, 2, 2, 8)
    fine = Mesh(devices, ("x", "yl", "c", "yh", "z"))
    ctx, head = ("x", "yl", "c"), ("yh", "z")
    tile = P(ctx, head)
    return jax.shard_map(
        on_device,
        mesh=fine,
        in_specs=(tile, tile, tile, tile, P(ctx + head, None), P()),
        out_specs=(tile, tile, tile),
        check_vma=False,
    )
```

```python
import functools
import math

import jax
import jax.numpy as jnp
from jax import lax
from jax.experimental import pallas as pl
from jax.experimental.pallas import tpu as pltpu
from jax.sharding import Mesh, PartitionSpec as P

HD = 112
W = 128
NX = 4
BLK = 160
OWN = 2 * BLK
QT = 256
QROWS = NX * OWN
NQT = QROWS // QT
HALF = 16 * BLK
SKC = 512
SPER = 5
GKC = 320
GPER = 6
DROWS = QROWS + QT
SCALE = 1.0 / math.sqrt(HD)
LOG2E = math.log2(math.e)
CEXP = SCALE * LOG2E
NEG = -1e30
LIMIT = 56 * 1024 * 1024
F32 = jnp.float32
BF16 = jnp.bfloat16

VM = pl.BlockSpec(memory_space=pltpu.VMEM)
SM = pl.BlockSpec(memory_space=pltpu.SMEM)


def call(kernel, outs, scratch, name, after=0):
    def run(*args):
        specs = [SM if a.dtype == jnp.int32 or a.size <= 8 else VM for a in args]
        if after:
            specs[-after:] = [pl.BlockSpec(memory_space=pl.ANY)] * after
        return pl.pallas_call(
            kernel,
            out_shape=[jax.ShapeDtypeStruct(s, d) for s, d in outs],
            in_specs=specs,
            out_specs=[VM] * len(outs),
            scratch_shapes=scratch,
            compiler_params=pltpu.CompilerParams(vmem_limit_bytes=LIMIT),
            name=name,
        )(*args)

    return run


def ctx_of(ids, s, dyl, dc):
    x = lax.rem(ids[0] + (NX - s), NX)
    yl = ids[1] if dyl == 0 else 1 - ids[1]
    c = ids[2] if dc == 0 else 1 - ids[2]
    return x * 4 + yl * 2 + c


def cotangent_pack_kernel(d_ref, out_ref):
    out_ref[:, :, HD:] = jnp.zeros((64, 20, W - HD), BF16)
    for n in range(64):
        out_ref[(n % NX) * 16 + n // NX, :, :HD] = d_ref[:, n * HD : (n + 1) * HD]


def here():
    return lax.axis_index("x"), lax.axis_index("yl"), lax.axis_index("c")


def key_columns(plan):
    ctx = ctx_of(here(), 0, 0, 0)
    row = lax.broadcasted_iota(jnp.int32, (OWN, W - HD), 0)
    lane = lax.broadcasted_iota(jnp.int32, (OWN, W - HD), 1)
    first, second = plan[2 * ctx] * BLK, plan[2 * ctx + 1] * BLK
    pos = jnp.where(row < BLK, first + row, second + row - BLK)
    high = (pos // 64) * 64
    one = jnp.where(lane < 9, 1, 0)
    return jnp.where(lane < 3, high, jnp.where(lane < 6, pos - high, one)).astype(F32).astype(BF16)


def pack_kernel(extras, plan, a_ref, b_ref, *rest):
    outs, buf = rest[-5:-1], rest[-1]
    if extras == "kv":
        lane = lax.broadcasted_iota(jnp.int32, (OWN, W - HD), 1)
        wide = (key_columns(plan), jnp.where(lane < 3, 1.0, 0.0).astype(BF16))
    else:
        wide = (jnp.zeros((OWN, W - HD), BF16),) * 2
    for n in range(NX):
        for i, ref in enumerate((a_ref, b_ref)):
            rows = slice(i * OWN, (i + 1) * OWN)
            buf[n, rows, :HD] = ref[:, n * HD : (n + 1) * HD]
            buf[n, rows, HD:] = wide[i]
    x = lax.axis_index("x")
    for s in range(NX):
        outs[s][...] = buf[lax.rem(x + s, NX)]


def at(start, size):
    return pl.ds(pl.multiple_of(start, 32), size)


def split3(value):
    a = value.astype(BF16)
    r = value - a.astype(F32)
    b = r.astype(BF16)
    return a, b, (r - b.astype(F32)).astype(BF16)


def sort_keys(ids, tables, row, dyl, first, pieces, swapped, dst):
    for s in range(NX):
        for dc in range(2):
            ctx = ctx_of(ids, s, dyl, dc)
            near, far = (pieces, swapped)[dc]
            src, base = (near, 0) if s == 0 else (far, 2 * (s - 1) * OWN)
            for h in range(2):
                begin = base + first + h * BLK
                dst[at(tables[row, 2 * ctx + h] * BLK, BLK), :] = src[begin : begin + BLK, :]


def sort_rows(ids, tables, blocks, dst):
    for s in range(NX):
        ctx = ctx_of(ids, s, 0, 0)
        for h in range(2):
            dst[at(tables[1, 2 * ctx + h] * BLK, BLK), :] = blocks(s, h)


def sort_limits(ids, tables, limits):
    for s in range(NX):
        ctx = ctx_of(ids, s, 0, 0)
        for h in range(2):
            r = tables[1, 2 * ctx + h]
            limits[0, r] = tables[0, 2 * ctx + h]
            limits[1, r] = tables[2, 2 * ctx + h]
            limits[2, r] = tables[3, 2 * ctx + h]


def tile_limits(limits, i, dyl):
    b0, b1 = (QT * i) // BLK, (QT * i + QT - 1) // BLK
    row = lax.broadcasted_iota(jnp.int32, (1, QT), 1) + QT * i
    lim = jnp.zeros((1, QT), jnp.int32)
    for b in range(b0, b1 + 1):
        inside = jnp.logical_and(row >= b * BLK, row < (b + 1) * BLK)
        if dyl == 1:
            value = jnp.broadcast_to(limits[1, b] * BLK - 1, (1, QT))
        else:
            value = limits[dyl, b] * BLK + (row - b * BLK)
        lim = jnp.where(inside, value, lim)
    return lim, limits[dyl, b1] * BLK + (0 if dyl == 1 else BLK)


def list_work(limits, dyl, size, per, work, lims):
    count = jnp.int32(0)
    for i in range(NQT):
        lim, last = tile_limits(limits, i, dyl)
        lims[i] = lim
        n = lax.div(last + size - 1, size)

        def put(k, carry, i=i, count=count):
            work[0, count + k] = i
            work[1, count + k] = k
            return carry

        lax.fori_loop(0, n, put, 0)
        count = count + n
    lims[NQT] = jnp.full((1, QT), -1, jnp.int32)
    for u in range(per - 1):
        work[0, count + u] = NQT
        work[1, count + u] = 0
    return lax.div(count + per - 1, per)


def stats_kernel(tables, slope, *rest):
    ids = here()
    qo, kv, kv_c, kv_y, kv_yc = rest[0:4], rest[4:6], rest[6:8], rest[8:10], rest[10:12]
    qs, qt = rest[12:14]
    keys, limits, work, lims, tops, totals = rest[14:20]
    sort_keys(ids, tables, 3, 0, 0, kv, kv_c, keys)
    sort_keys(ids, tables, 3, 1, 0, kv_y, kv_yc, keys)
    sort_rows(ids, tables, lambda s, h: qo[s][h * BLK : (h + 1) * BLK, :], qs)
    qs[QROWS:, :] = jnp.zeros((QT, W), BF16)
    sort_limits(ids, tables, limits)
    m1, m2, m3 = split3(jnp.full((1, QT), slope[0] / SCALE, F32))
    for i in range(NQT):
        qt[i] = qs[i * QT : (i + 1) * QT, :].T
        qt[i, HD : HD + 16, :] = jnp.concatenate(
            [m1, m2, m3, m1, m2, m3, jnp.zeros((10, QT), BF16)], axis=0
        )
    qt[NQT] = jnp.zeros((W, QT), BF16)
    steps = list_work(limits, 2, SKC, SPER, work, lims)
    tops[...] = jnp.full(tops.shape, NEG, F32)
    totals[...] = jnp.zeros(totals.shape, F32)

    def step(j, carry):
        for u in range(SPER):
            item = j * SPER + u
            tile, chunk = work[0, item], work[1, item]
            s = jnp.dot(keys[at(chunk * SKC, SKC), :], qt[tile], preferred_element_type=F32)
            index = lax.broadcasted_iota(jnp.int32, (SKC, QT), 0)
            s = jnp.where(index <= lims[tile] - chunk * SKC, s, NEG)
            s = s.reshape(SKC // 8, 8, QT)
            top = jnp.max(s, axis=0)
            tops[tile, chunk] = top
            totals[tile, chunk] = jnp.sum(jnp.exp2((s - top[None]) * CEXP), axis=0)
        return carry

    lax.fori_loop(0, steps, step, 0)
    for i in range(NQT):
        top = jnp.max(jnp.max(tops[i], axis=0), axis=0, keepdims=True)
        total8 = jnp.sum(totals[i] * jnp.exp2((tops[i] - top) * CEXP), axis=0)
        total = jnp.sum(total8, axis=0, keepdims=True)
        l1, l2, l3 = split3(-(top + jnp.log(total) * (1.0 / SCALE)))
        qt[i, HD : HD + 16, :] = jnp.concatenate(
            [m1, m2, m3, m1, m2, m3, l1, l2, l3, jnp.zeros((7, QT), BF16)], axis=0
        )


def grads_loop(dyl, keys, vals, qs, qt, dos, dot, limits, dkey, dval, dq, work, lims):
    dkey[...] = jnp.zeros((HALF, W), F32)
    dval[...] = jnp.zeros((HALF, W), F32)
    steps = list_work(limits, dyl, GKC, GPER, work, lims)

    def step(j, carry):
        items = []
        for u in range(GPER):
            item = j * GPER + u
            tile, chunk = work[0, item], work[1, item]
            rows = at(chunk * GKC, GKC)
            cols = at(tile * QT, QT)
            kc = keys[rows, :]
            s = jnp.dot(kc, qt[tile], preferred_element_type=F32)
            dp = jnp.dot(vals[rows, :], dot[tile], preferred_element_type=F32)
            items.append((tile, chunk, rows, cols, kc, s, dp))
        parts = []
        for tile, chunk, rows, cols, kc, s, dp in items:
            index = lax.broadcasted_iota(jnp.int32, (GKC, QT), 0)
            p = jnp.where(index <= lims[tile] - chunk * GKC, jnp.exp2(s * CEXP), 0.0)
            ds = (p * dp).astype(BF16)
            dv = jnp.dot(p.astype(BF16), dos[cols, :], preferred_element_type=F32)
            dk = jnp.dot(ds, qs[cols, :], preferred_element_type=F32)
            d = lax.dot_general(ds, kc, (((0,), (0,)), ((), ())), preferred_element_type=F32)
            parts.append((rows, cols, dv, dk, d))
        for rows, cols, dv, dk, d in parts:
            dval[rows, :] += dv
            dkey[rows, :] += dk
            dq[cols, :] += d
        return carry

    lax.fori_loop(0, steps, step, 0)


def unsort(ids, tables, dyl, dc, dkey, dval, out):
    for s in range(NX):
        ctx = ctx_of(ids, s, dyl, dc)
        for h in range(2):
            rows = at(tables[0, 2 * ctx + h] * BLK, BLK)
            base = s * 2 * OWN + h * BLK
            out[base : base + BLK, :] = (dkey[rows, :] * SCALE).astype(BF16)
            out[base + OWN : base + OWN + BLK, :] = dval[rows, :].astype(BF16)


def grads_other_kernel(tables, *rest):
    ids = here()
    qo, kv_y, kv_yc = rest[0:4], rest[4:6], rest[6:8]
    dor, qs, qt = rest[8:11]
    dos, dot, dq, keep, send = rest[11:16]
    keys, vals, dkey, dval, work, lims, flat, outs, limits = rest[16:25]
    sort_keys(ids, tables, 0, 1, 0, kv_y, kv_yc, keys)
    sort_keys(ids, tables, 0, 1, OWN, kv_y, kv_yc, vals)
    sort_limits(ids, tables, limits)
    for n in range(64):
        flat[n * 20 : (n + 1) * 20, :] = dor[n]

    def block(s, h):
        x = lax.rem(ids[0] + (NX - s), NX)
        return flat[at(x * OWN + h * BLK, BLK), :]

    sort_rows(ids, tables, block, dos)
    sort_rows(ids, tables, lambda s, h: qo[s][OWN + h * BLK : OWN + (h + 1) * BLK, :], outs)
    for i in range(NQT):
        cols = slice(i * QT, (i + 1) * QT)
        prod = dos[cols, :].astype(F32) * outs[cols, :].astype(F32)
        delta = jnp.sum(prod.T, axis=0, keepdims=True)
        d1, d2, d3 = split3(-delta)
        dot[i] = dos[cols, :].T
        dot[i, HD : HD + 16, :] = jnp.concatenate(
            [d1, d2, d3, jnp.zeros((13, QT), BF16)], axis=0
        )
    dot[NQT] = jnp.zeros((W, QT), BF16)
    dos[QROWS:, :] = jnp.zeros((QT, W), BF16)
    dq[...] = jnp.zeros((DROWS, W), F32)
    grads_loop(1, keys, vals, qs, qt, dos, dot, limits, dkey, dval, dq, work, lims)
    unsort(ids, tables, 1, 0, dkey, dval, keep)
    unsort(ids, tables, 1, 1, dkey, dval, send)


def grads_own_kernel(tables, *rest):
    ids = here()
    kv, kv_c = rest[0:2], rest[2:4]
    qs, qt, dos, dot, dq_in = rest[4:9]
    dqo, keep, send = rest[9:13], rest[13], rest[14]
    keys, vals, dkey, dval, work, lims, dq, limits = rest[15:23]
    sort_keys(ids, tables, 0, 0, 0, kv, kv_c, keys)
    sort_keys(ids, tables, 0, 0, OWN, kv, kv_c, vals)
    sort_limits(ids, tables, limits)
    dq[...] = dq_in[...]
    grads_loop(0, keys, vals, qs, qt, dos, dot, limits, dkey, dval, dq, work, lims)
    unsort(ids, tables, 0, 0, dkey, dval, keep)
    unsort(ids, tables, 0, 1, dkey, dval, send)
    for s in range(NX):
        ctx = ctx_of(ids, s, 0, 0)
        for h in range(2):
            rows = at(tables[1, 2 * ctx + h] * BLK, BLK)
            dqo[s][h * BLK : (h + 1) * BLK, :] = (dq[rows, :] * SCALE).astype(BF16)


def add_kernel(a, b, out):
    out[...] = (a[...].astype(F32) + b[...].astype(F32)).astype(BF16)


def add_own_kernel(a, b, c, *outs):
    for s in range(NX):
        rows = slice(s * 2 * OWN, (s + 1) * 2 * OWN)
        total = a[rows, :].astype(F32) + b[rows, :].astype(F32) + c[rows, :].astype(F32)
        outs[s][...] = total.astype(BF16)


def unpack_kernel(*rest):
    dqs, dkvs, outs, buf = rest[0:4], rest[4:8], rest[8:11], rest[11]
    x = lax.axis_index("x")
    for s in range(NX):
        head = lax.rem(x + s, NX)
        buf[head, :OWN, :] = dqs[s][...]
        buf[head, OWN:, :] = dkvs[s][...]
    for n in range(NX):
        for i in range(3):
            outs[i][:, n * HD : (n + 1) * HD] = buf[n, i * OWN : (i + 1) * OWN, :HD]


def shift(value, by, flip=False):
    pairs = []
    for x in range(NX):
        for yl in range(2):
            pairs.append((2 * x + yl, 2 * ((x + by) % NX) + (1 - yl if flip else yl)))
    return lax.ppermute(value, ("x", "yl"), pairs)


def swap_core(value):
    return lax.ppermute(value, "c", [(0, 1), (1, 0)])


def worklist(size, keys, per):
    items = NQT * (keys // size) + per
    return [pltpu.SMEM((2, items), jnp.int32), pltpu.VMEM((NQT + 1, 1, QT), jnp.int32)]


def plan_tables(plan):
    block = jnp.arange(32, dtype=jnp.int32)
    half = (block >> 2) & 1
    group = (block >> 1) & 3
    before = plan[None, :] < plan[:, None]
    same_half = half[None, :] == half[:, None]
    same_group = group[None, :] == group[:, None]

    def count(m):
        return jnp.sum(jnp.where(jnp.logical_and(before, m), 1, 0), axis=1, dtype=jnp.int32)

    return jnp.stack([count(same_half), count(same_group), count(jnp.logical_not(same_half)), plan])


def on_device(queries, keys, values, out_fwd, d_out, plan):
    piece = ((2 * OWN, W), BF16)
    stack = ((NX * 2 * OWN, W), BF16)
    x = lax.axis_index("x")
    tables = plan_tables(plan)
    head_id = (lax.axis_index("yh") * 8 + lax.axis_index("z")) * NX + x
    slope = jnp.exp2(-8.0 * (head_id + 1).astype(F32) / 64.0).reshape(1)

    buf = [pltpu.VMEM((NX, 2 * OWN, W), BF16)]
    kv = call(functools.partial(pack_kernel, "kv"), [piece] * 4, buf, "pack_kv")(plan, keys, values)
    kv, d_out = lax.optimization_barrier((kv, d_out))
    (d_pack,) = call(cotangent_pack_kernel, [((64, 20, W), BF16)], [], "cotangent_pack")(d_out)
    d_rows = lax.all_to_all(d_pack, ("x", "yh", "z"), 0, 0)
    kv = [kv[0], jnp.concatenate([shift(kv[s], s) for s in (1, 2, 3)])]
    kv_y = [shift(a, 0, True) for a in kv]
    kv_c = [swap_core(a) for a in kv]
    qo = call(functools.partial(pack_kernel, "qo"), [piece] * 4, buf, "pack_qo", 2)(
        plan, queries, out_fwd, kv[1], tables
    )
    qo = [qo[0]] + [shift(qo[s], s) for s in (1, 2, 3)]
    kv_y, qo, d_rows = lax.optimization_barrier((kv_y, qo, d_rows))
    kv_yc = [swap_core(a) for a in kv_y]

    limits = pltpu.SMEM((3, 8), jnp.int32)
    qs, qt = call(
        stats_kernel,
        [((DROWS, W), BF16), ((NQT + 1, W, QT), BF16)],
        [pltpu.VMEM((2 * HALF, W), BF16), limits]
        + worklist(SKC, 2 * HALF, SPER)
        + [pltpu.VMEM((NQT + 1, 2 * HALF // SKC, 8, QT), F32)] * 2,
        "stats",
    )(tables, slope, *qo, *kv, *kv_c, *kv_y, *kv_yc)
    accs = [pltpu.VMEM((HALF, W), BF16)] * 2 + [pltpu.VMEM((HALF, W), F32)] * 2
    accs = accs + worklist(GKC, HALF, GPER)
    dos, dot, dq, keep, send = call(
        grads_other_kernel,
        [((DROWS, W), BF16), ((NQT + 1, W, QT), BF16), ((DROWS, W), F32), stack, stack],
        accs + [pltpu.VMEM((QROWS, W), BF16)] * 2 + [limits],
        "grads_other",
    )(tables, *qo, *kv_y, *kv_yc, d_rows, qs, qt)
    (dkv_y,) = call(add_kernel, [stack], [], "add_other")(keep, swap_core(send))
    dq, dkv_y = lax.optimization_barrier((dq, dkv_y))
    dkv_y = shift(dkv_y, 0, True)

    *dqs, keep, send = call(
        grads_own_kernel,
        [((OWN, W), BF16)] * 4 + [stack, stack],
        accs + [pltpu.VMEM((DROWS, W), F32), limits],
        "grads_own",
    )(tables, *kv, *kv_c, qs, qt, dos, dot, dq)
    dqs[1], dqs[2], dkv_y = lax.optimization_barrier((dqs[1], dqs[2], dkv_y))
    swapped = swap_core(send)
    dqs = [dqs[0]] + [shift(dqs[s], -s) for s in (1, 2, 3)]
    dkvs = call(add_own_kernel, [piece] * 4, [], "add_own")(keep, swapped, dkv_y)
    dkvs = [dkvs[0]] + [shift(dkvs[s], -s) for s in (1, 2, 3)]
    return tuple(
        call(
            unpack_kernel,
            [((OWN, NX * HD), BF16)] * 3,
            [pltpu.VMEM((NX, 3 * OWN, W), BF16)],
            "unpack",
        )(*dqs, *dkvs)
    )


def solution(mesh):
    devices = mesh.devices.reshape(4, 2, 2, 2, 8)
    fine = Mesh(devices, ("x", "yl", "c", "yh", "z"))
    ctx, head = ("x", "yl", "c"), ("yh", "z")
    tile = P(ctx, head)
    return jax.shard_map(
        on_device,
        mesh=fine,
        in_specs=(tile, tile, tile, tile, P(ctx + head, None), P()),
        out_specs=(tile, tile, tile),
        check_vma=False,
    )
```

```python
import functools
import math

import jax
import jax.numpy as jnp
from jax import lax
from jax.experimental import pallas as pl
from jax.experimental.pallas import tpu as pltpu
from jax.sharding import Mesh, PartitionSpec as P

HD = 112
W = 128
NX = 4
BLK = 160
OWN = 2 * BLK
QT = 256
QROWS = NX * OWN
NQT = QROWS // QT
HALF = 16 * BLK
SKC = 512
SPER = 5
GKC = 320
GPER = 6
DROWS = QROWS + QT
SCALE = 1.0 / math.sqrt(HD)
LOG2E = math.log2(math.e)
CEXP = SCALE * LOG2E
NEG = -1e30
LIMIT = 24 * 1024 * 1024
F32 = jnp.float32
BF16 = jnp.bfloat16

VM = pl.BlockSpec(memory_space=pltpu.VMEM)
SM = pl.BlockSpec(memory_space=pltpu.SMEM)


def call(kernel, outs, scratch, name, after=0):
    def run(*args):
        specs = [SM if a.dtype == jnp.int32 or a.size <= 8 else VM for a in args]
        if after:
            specs[-after:] = [pl.BlockSpec(memory_space=pl.ANY)] * after
        return pl.pallas_call(
            kernel,
            out_shape=[jax.ShapeDtypeStruct(s, d) for s, d in outs],
            in_specs=specs,
            out_specs=[VM] * len(outs),
            scratch_shapes=scratch,
            compiler_params=pltpu.CompilerParams(vmem_limit_bytes=LIMIT),
            name=name,
        )(*args)

    return run


def ctx_of(ids, s, dyl, dc):
    x = lax.rem(ids[0] + (NX - s), NX)
    yl = ids[1] if dyl == 0 else 1 - ids[1]
    c = ids[2] if dc == 0 else 1 - ids[2]
    return x * 4 + yl * 2 + c


def cotangent_pack_kernel(d_ref, out_ref):
    out_ref[:, :, HD:] = jnp.zeros((64, 20, W - HD), BF16)
    for n in range(64):
        out_ref[(n % NX) * 16 + n // NX, :, :HD] = d_ref[:, n * HD : (n + 1) * HD]


def here():
    return lax.axis_index("x"), lax.axis_index("yl"), lax.axis_index("c")


def key_columns(plan):
    ctx = ctx_of(here(), 0, 0, 0)
    row = lax.broadcasted_iota(jnp.int32, (OWN, W - HD), 0)
    lane = lax.broadcasted_iota(jnp.int32, (OWN, W - HD), 1)
    first, second = plan[2 * ctx] * BLK, plan[2 * ctx + 1] * BLK
    pos = jnp.where(row < BLK, first + row, second + row - BLK)
    high = (pos // 64) * 64
    one = jnp.where(lane < 9, 1, 0)
    return jnp.where(lane < 3, high, jnp.where(lane < 6, pos - high, one)).astype(F32).astype(BF16)


def pack_kernel(extras, plan, a_ref, b_ref, *rest):
    outs, buf = rest[-5:-1], rest[-1]
    if extras == "kv":
        lane = lax.broadcasted_iota(jnp.int32, (OWN, W - HD), 1)
        wide = (key_columns(plan), jnp.where(lane < 3, 1.0, 0.0).astype(BF16))
    else:
        wide = (jnp.zeros((OWN, W - HD), BF16),) * 2
    for n in range(NX):
        for i, ref in enumerate((a_ref, b_ref)):
            rows = slice(i * OWN, (i + 1) * OWN)
            buf[n, rows, :HD] = ref[:, n * HD : (n + 1) * HD]
            buf[n, rows, HD:] = wide[i]
    x = lax.axis_index("x")
    for s in range(NX):
        outs[s][...] = buf[lax.rem(x + s, NX)]


def at(start, size):
    return pl.ds(pl.multiple_of(start, 32), size)


def split3(value):
    a = value.astype(BF16)
    r = value - a.astype(F32)
    b = r.astype(BF16)
    return a, b, (r - b.astype(F32)).astype(BF16)


def sort_keys(ids, tables, row, dyl, first, pieces, swapped, dst):
    for s in range(NX):
        for dc in range(2):
            ctx = ctx_of(ids, s, dyl, dc)
            near, far = (pieces, swapped)[dc]
            src, base = (near, 0) if s == 0 else (far, 2 * (s - 1) * OWN)
            for h in range(2):
                begin = base + first + h * BLK
                dst[at(tables[row, 2 * ctx + h] * BLK, BLK), :] = src[begin : begin + BLK, :]


def sort_rows(ids, tables, blocks, dst):
    for s in range(NX):
        ctx = ctx_of(ids, s, 0, 0)
        for h in range(2):
            dst[at(tables[1, 2 * ctx + h] * BLK, BLK), :] = blocks(s, h)


def sort_limits(ids, tables, limits):
    for s in range(NX):
        ctx = ctx_of(ids, s, 0, 0)
        for h in range(2):
            r = tables[1, 2 * ctx + h]
            limits[0, r] = tables[0, 2 * ctx + h]
            limits[1, r] = tables[2, 2 * ctx + h]
            limits[2, r] = tables[3, 2 * ctx + h]


def tile_limits(limits, i, dyl):
    b0, b1 = (QT * i) // BLK, (QT * i + QT - 1) // BLK
    row = lax.broadcasted_iota(jnp.int32, (1, QT), 1) + QT * i
    lim = jnp.zeros((1, QT), jnp.int32)
    for b in range(b0, b1 + 1):
        inside = jnp.logical_and(row >= b * BLK, row < (b + 1) * BLK)
        if dyl == 1:
            value = jnp.broadcast_to(limits[1, b] * BLK - 1, (1, QT))
        else:
            value = limits[dyl, b] * BLK + (row - b * BLK)
        lim = jnp.where(inside, value, lim)
    return lim, limits[dyl, b1] * BLK + (0 if dyl == 1 else BLK)


def list_work(limits, dyl, size, per, work, lims):
    count = jnp.int32(0)
    for i in range(NQT):
        lim, last = tile_limits(limits, i, dyl)
        lims[i] = lim
        n = lax.div(last + size - 1, size)

        def put(k, carry, i=i, count=count):
            work[0, count + k] = i
            work[1, count + k] = k
            return carry

        lax.fori_loop(0, n, put, 0)
        count = count + n
    lims[NQT] = jnp.full((1, QT), -1, jnp.int32)
    for u in range(per - 1):
        work[0, count + u] = NQT
        work[1, count + u] = 0
    return lax.div(count + per - 1, per)


def stats_kernel(tables, slope, *rest):
    ids = here()
    qo, kv, kv_c, kv_y, kv_yc = rest[0:4], rest[4:6], rest[6:8], rest[8:10], rest[10:12]
    qs, qt = rest[12:14]
    keys, limits, work, lims, tops, totals = rest[14:20]
    sort_keys(ids, tables, 3, 0, 0, kv, kv_c, keys)
    sort_keys(ids, tables, 3, 1, 0, kv_y, kv_yc, keys)
    sort_rows(ids, tables, lambda s, h: qo[s][h * BLK : (h + 1) * BLK, :], qs)
    qs[QROWS:, :] = jnp.zeros((QT, W), BF16)
    sort_limits(ids, tables, limits)
    m1, m2, m3 = split3(jnp.full((1, QT), slope[0] / SCALE, F32))
    for i in range(NQT):
        qt[i] = qs[i * QT : (i + 1) * QT, :].T
        qt[i, HD : HD + 16, :] = jnp.concatenate(
            [m1, m2, m3, m1, m2, m3, jnp.zeros((10, QT), BF16)], axis=0
        )
    qt[NQT] = jnp.zeros((W, QT), BF16)
    steps = list_work(limits, 2, SKC, SPER, work, lims)
    tops[...] = jnp.full(tops.shape, NEG, F32)
    totals[...] = jnp.zeros(totals.shape, F32)

    def step(j, carry):
        for u in range(SPER):
            item = j * SPER + u
            tile, chunk = work[0, item], work[1, item]
            s = jnp.dot(keys[at(chunk * SKC, SKC), :], qt[tile], preferred_element_type=F32)
            index = lax.broadcasted_iota(jnp.int32, (SKC, QT), 0)
            s = jnp.where(index <= lims[tile] - chunk * SKC, s, NEG)
            s = s.reshape(SKC // 8, 8, QT)
            top = jnp.max(s, axis=0)
            tops[tile, chunk] = top
            totals[tile, chunk] = jnp.sum(jnp.exp2((s - top[None]) * CEXP), axis=0)
        return carry

    lax.fori_loop(0, steps, step, 0)
    for i in range(NQT):
        top = jnp.max(jnp.max(tops[i], axis=0), axis=0, keepdims=True)
        total8 = jnp.sum(totals[i] * jnp.exp2((tops[i] - top) * CEXP), axis=0)
        total = jnp.sum(total8, axis=0, keepdims=True)
        l1, l2, l3 = split3(-(top + jnp.log(total) * (1.0 / SCALE)))
        qt[i, HD : HD + 16, :] = jnp.concatenate(
            [m1, m2, m3, m1, m2, m3, l1, l2, l3, jnp.zeros((7, QT), BF16)], axis=0
        )


def grads_loop(dyl, keys, vals, qs, qt, dos, dot, limits, dkey, dval, dq, work, lims):
    dkey[...] = jnp.zeros((HALF, W), F32)
    dval[...] = jnp.zeros((HALF, W), F32)
    steps = list_work(limits, dyl, GKC, GPER, work, lims)

    def step(j, carry):
        items = []
        for u in range(GPER):
            item = j * GPER + u
            tile, chunk = work[0, item], work[1, item]
            rows = at(chunk * GKC, GKC)
            cols = at(tile * QT, QT)
            kc = keys[rows, :]
            s = jnp.dot(kc, qt[tile], preferred_element_type=F32)
            dp = jnp.dot(vals[rows, :], dot[tile], preferred_element_type=F32)
            items.append((tile, chunk, rows, cols, kc, s, dp))
        parts = []
        for tile, chunk, rows, cols, kc, s, dp in items:
            index = lax.broadcasted_iota(jnp.int32, (GKC, QT), 0)
            p = jnp.where(index <= lims[tile] - chunk * GKC, jnp.exp2(s * CEXP), 0.0)
            ds = (p * dp).astype(BF16)
            dv = jnp.dot(p.astype(BF16), dos[cols, :], preferred_element_type=F32)
            dk = jnp.dot(ds, qs[cols, :], preferred_element_type=F32)
            d = lax.dot_general(ds, kc, (((0,), (0,)), ((), ())), preferred_element_type=F32)
            parts.append((rows, cols, dv, dk, d))
        for rows, cols, dv, dk, d in parts:
            dval[rows, :] += dv
            dkey[rows, :] += dk
            dq[cols, :] += d
        return carry

    lax.fori_loop(0, steps, step, 0)


def unsort(ids, tables, dyl, dc, dkey, dval, out):
    for s in range(NX):
        ctx = ctx_of(ids, s, dyl, dc)
        for h in range(2):
            rows = at(tables[0, 2 * ctx + h] * BLK, BLK)
            base = s * 2 * OWN + h * BLK
            out[base : base + BLK, :] = (dkey[rows, :] * SCALE).astype(BF16)
            out[base + OWN : base + OWN + BLK, :] = dval[rows, :].astype(BF16)


def grads_other_kernel(tables, *rest):
    ids = here()
    qo, kv_y, kv_yc = rest[0:4], rest[4:6], rest[6:8]
    dor, qs, qt = rest[8:11]
    dos, dot, dq, keep, send = rest[11:16]
    keys, vals, dkey, dval, work, lims, flat, outs, limits = rest[16:25]
    sort_keys(ids, tables, 0, 1, 0, kv_y, kv_yc, keys)
    sort_keys(ids, tables, 0, 1, OWN, kv_y, kv_yc, vals)
    sort_limits(ids, tables, limits)
    for n in range(64):
        flat[n * 20 : (n + 1) * 20, :] = dor[n]

    def block(s, h):
        x = lax.rem(ids[0] + (NX - s), NX)
        return flat[at(x * OWN + h * BLK, BLK), :]

    sort_rows(ids, tables, block, dos)
    sort_rows(ids, tables, lambda s, h: qo[s][OWN + h * BLK : OWN + (h + 1) * BLK, :], outs)
    for i in range(NQT):
        cols = slice(i * QT, (i + 1) * QT)
        prod = dos[cols, :].astype(F32) * outs[cols, :].astype(F32)
        delta = jnp.sum(prod.T, axis=0, keepdims=True)
        d1, d2, d3 = split3(-delta)
        dot[i] = dos[cols, :].T
        dot[i, HD : HD + 16, :] = jnp.concatenate(
            [d1, d2, d3, jnp.zeros((13, QT), BF16)], axis=0
        )
    dot[NQT] = jnp.zeros((W, QT), BF16)
    dos[QROWS:, :] = jnp.zeros((QT, W), BF16)
    dq[...] = jnp.zeros((DROWS, W), F32)
    grads_loop(1, keys, vals, qs, qt, dos, dot, limits, dkey, dval, dq, work, lims)
    unsort(ids, tables, 1, 0, dkey, dval, keep)
    unsort(ids, tables, 1, 1, dkey, dval, send)


def grads_own_kernel(tables, *rest):
    ids = here()
    kv, kv_c = rest[0:2], rest[2:4]
    qs, qt, dos, dot, dq_in = rest[4:9]
    dqo, keep, send = rest[9:13], rest[13], rest[14]
    keys, vals, dkey, dval, work, lims, dq, limits = rest[15:23]
    sort_keys(ids, tables, 0, 0, 0, kv, kv_c, keys)
    sort_keys(ids, tables, 0, 0, OWN, kv, kv_c, vals)
    sort_limits(ids, tables, limits)
    dq[...] = dq_in[...]
    grads_loop(0, keys, vals, qs, qt, dos, dot, limits, dkey, dval, dq, work, lims)
    unsort(ids, tables, 0, 0, dkey, dval, keep)
    unsort(ids, tables, 0, 1, dkey, dval, send)
    for s in range(NX):
        ctx = ctx_of(ids, s, 0, 0)
        for h in range(2):
            rows = at(tables[1, 2 * ctx + h] * BLK, BLK)
            dqo[s][h * BLK : (h + 1) * BLK, :] = (dq[rows, :] * SCALE).astype(BF16)


def add_kernel(a, b, out):
    out[...] = (a[...].astype(F32) + b[...].astype(F32)).astype(BF16)


def add_own_kernel(a, b, c, *outs):
    for s in range(NX):
        rows = slice(s * 2 * OWN, (s + 1) * 2 * OWN)
        total = a[rows, :].astype(F32) + b[rows, :].astype(F32) + c[rows, :].astype(F32)
        outs[s][...] = total.astype(BF16)


def unpack_kernel(*rest):
    dqs, dkvs, outs, buf = rest[0:4], rest[4:8], rest[8:11], rest[11]
    x = lax.axis_index("x")
    for s in range(NX):
        head = lax.rem(x + s, NX)
        buf[head, :OWN, :] = dqs[s][...]
        buf[head, OWN:, :] = dkvs[s][...]
    for n in range(NX):
        for i in range(3):
            outs[i][:, n * HD : (n + 1) * HD] = buf[n, i * OWN : (i + 1) * OWN, :HD]


def shift(value, by, flip=False):
    pairs = []
    for x in range(NX):
        for yl in range(2):
            pairs.append((2 * x + yl, 2 * ((x + by) % NX) + (1 - yl if flip else yl)))
    return lax.ppermute(value, ("x", "yl"), pairs)


def swap_core(value):
    return lax.ppermute(value, "c", [(0, 1), (1, 0)])


def worklist(size, keys, per):
    items = NQT * (keys // size) + per
    return [pltpu.SMEM((2, items), jnp.int32), pltpu.VMEM((NQT + 1, 1, QT), jnp.int32)]


def plan_tables(plan):
    block = jnp.arange(32, dtype=jnp.int32)
    half = (block >> 2) & 1
    group = (block >> 1) & 3
    before = plan[None, :] < plan[:, None]
    same_half = half[None, :] == half[:, None]
    same_group = group[None, :] == group[:, None]

    def count(m):
        return jnp.sum(jnp.where(jnp.logical_and(before, m), 1, 0), axis=1, dtype=jnp.int32)

    return jnp.stack([count(same_half), count(same_group), count(jnp.logical_not(same_half)), plan])


def on_device(queries, keys, values, out_fwd, d_out, plan):
    piece = ((2 * OWN, W), BF16)
    stack = ((NX * 2 * OWN, W), BF16)
    x = lax.axis_index("x")
    tables = plan_tables(plan)
    head_id = (lax.axis_index("yh") * 8 + lax.axis_index("z")) * NX + x
    slope = jnp.exp2(-8.0 * (head_id + 1).astype(F32) / 64.0).reshape(1)

    buf = [pltpu.VMEM((NX, 2 * OWN, W), BF16)]
    kv = call(functools.partial(pack_kernel, "kv"), [piece] * 4, buf, "pack_kv")(plan, keys, values)
    kv, d_out = lax.optimization_barrier((kv, d_out))
    (d_pack,) = call(cotangent_pack_kernel, [((64, 20, W), BF16)], [], "cotangent_pack")(d_out)
    d_rows = lax.all_to_all(d_pack, ("x", "yh", "z"), 0, 0)
    kv = [kv[0], jnp.concatenate([shift(kv[s], s) for s in (1, 2, 3)])]
    kv_y = [shift(a, 0, True) for a in kv]
    kv_c = [swap_core(a) for a in kv]
    qo = call(functools.partial(pack_kernel, "qo"), [piece] * 4, buf, "pack_qo", 2)(
        plan, queries, out_fwd, kv[1], tables
    )
    qo = [qo[0]] + [shift(qo[s], s) for s in (1, 2, 3)]
    kv_y, qo, d_rows = lax.optimization_barrier((kv_y, qo, d_rows))
    kv_yc = [swap_core(a) for a in kv_y]

    limits = pltpu.SMEM((3, 8), jnp.int32)
    qs, qt = call(
        stats_kernel,
        [((DROWS, W), BF16), ((NQT + 1, W, QT), BF16)],
        [pltpu.VMEM((2 * HALF, W), BF16), limits]
        + worklist(SKC, 2 * HALF, SPER)
        + [pltpu.VMEM((NQT + 1, 2 * HALF // SKC, 8, QT), F32)] * 2,
        "stats",
    )(tables, slope, *qo, *kv, *kv_c, *kv_y, *kv_yc)
    accs = [pltpu.VMEM((HALF, W), BF16)] * 2 + [pltpu.VMEM((HALF, W), F32)] * 2
    accs = accs + worklist(GKC, HALF, GPER)
    dos, dot, dq, keep, send = call(
        grads_other_kernel,
        [((DROWS, W), BF16), ((NQT + 1, W, QT), BF16), ((DROWS, W), F32), stack, stack],
        accs + [pltpu.VMEM((QROWS, W), BF16)] * 2 + [limits],
        "grads_other",
    )(tables, *qo, *kv_y, *kv_yc, d_rows, qs, qt)
    (dkv_y,) = call(add_kernel, [stack], [], "add_other")(keep, swap_core(send))
    dq, dkv_y = lax.optimization_barrier((dq, dkv_y))
    dkv_y = shift(dkv_y, 0, True)

    *dqs, keep, send = call(
        grads_own_kernel,
        [((OWN, W), BF16)] * 4 + [stack, stack],
        accs + [pltpu.VMEM((DROWS, W), F32), limits],
        "grads_own",
    )(tables, *kv, *kv_c, qs, qt, dos, dot, dq)
    dqs[1], dqs[2], dkv_y = lax.optimization_barrier((dqs[1], dqs[2], dkv_y))
    swapped = swap_core(send)
    dqs = [dqs[0]] + [shift(dqs[s], -s) for s in (1, 2, 3)]
    dkvs = call(add_own_kernel, [piece] * 4, [], "add_own")(keep, swapped, dkv_y)
    dkvs = [dkvs[0]] + [shift(dkvs[s], -s) for s in (1, 2, 3)]
    return tuple(
        call(
            unpack_kernel,
            [((OWN, NX * HD), BF16)] * 3,
            [pltpu.VMEM((NX, 3 * OWN, W), BF16)],
            "unpack",
        )(*dqs, *dkvs)
    )


def solution(mesh):
    devices = mesh.devices.reshape(4, 2, 2, 2, 8)
    fine = Mesh(devices, ("x", "yl", "c", "yh", "z"))
    ctx, head = ("x", "yl", "c"), ("yh", "z")
    tile = P(ctx, head)
    return jax.shard_map(
        on_device,
        mesh=fine,
        in_specs=(tile, tile, tile, tile, P(ctx + head, None), P()),
        out_specs=(tile, tile, tile),
        check_vma=False,
    )
```

```python
import functools
import math

import jax
import jax.numpy as jnp
from jax import lax
from jax.experimental import pallas as pl
from jax.experimental.pallas import tpu as pltpu
from jax.sharding import Mesh, PartitionSpec as P

HD = 112
W = 128
NX = 4
BLK = 160
OWN = 2 * BLK
QT = 256
QROWS = NX * OWN
NQT = QROWS // QT
HALF = 16 * BLK
SKC = 512
SPER = 5
GKC = 320
GPER = 6
DROWS = QROWS + QT
SCALE = 1.0 / math.sqrt(HD)
LOG2E = math.log2(math.e)
CEXP = SCALE * LOG2E
NEG = -1e30
LIMIT = 24 * 1024 * 1024
F32 = jnp.float32
BF16 = jnp.bfloat16

VM = pl.BlockSpec(memory_space=pltpu.VMEM)
SM = pl.BlockSpec(memory_space=pltpu.SMEM)


def call(kernel, outs, scratch, name, after=0):
    def run(*args):
        specs = [SM if a.dtype == jnp.int32 or a.size <= 8 else VM for a in args]
        if after:
            specs[-after:] = [pl.BlockSpec(memory_space=pl.ANY)] * after
        return pl.pallas_call(
            kernel,
            out_shape=[jax.ShapeDtypeStruct(s, d) for s, d in outs],
            in_specs=specs,
            out_specs=[VM] * len(outs),
            scratch_shapes=scratch,
            compiler_params=pltpu.CompilerParams(vmem_limit_bytes=LIMIT),
            name=name,
        )(*args)

    return run


def ctx_of(ids, s, dyl, dc):
    x = lax.rem(ids[0] + (NX - s), NX)
    yl = ids[1] if dyl == 0 else 1 - ids[1]
    c = ids[2] if dc == 0 else 1 - ids[2]
    return x * 4 + yl * 2 + c


def cotangent_pack_kernel(d_ref, out_ref):
    out_ref[:, :, HD:] = jnp.zeros((64, 20, W - HD), BF16)
    for n in range(64):
        out_ref[(n % NX) * 16 + n // NX, :, :HD] = d_ref[:, n * HD : (n + 1) * HD]


def here():
    return lax.axis_index("x"), lax.axis_index("yl"), lax.axis_index("c")


def key_columns(plan):
    ctx = ctx_of(here(), 0, 0, 0)
    row = lax.broadcasted_iota(jnp.int32, (OWN, W - HD), 0)
    lane = lax.broadcasted_iota(jnp.int32, (OWN, W - HD), 1)
    first, second = plan[2 * ctx] * BLK, plan[2 * ctx + 1] * BLK
    pos = jnp.where(row < BLK, first + row, second + row - BLK)
    high = (pos // 64) * 64
    one = jnp.where(lane < 9, 1, 0)
    return jnp.where(lane < 3, high, jnp.where(lane < 6, pos - high, one)).astype(F32).astype(BF16)


def pack_kernel(extras, plan, a_ref, b_ref, *rest):
    outs, buf = rest[-5:-1], rest[-1]
    if extras == "kv":
        lane = lax.broadcasted_iota(jnp.int32, (OWN, W - HD), 1)
        wide = (key_columns(plan), jnp.where(lane < 3, 1.0, 0.0).astype(BF16))
    else:
        wide = (jnp.zeros((OWN, W - HD), BF16),) * 2
    for n in range(NX):
        for i, ref in enumerate((a_ref, b_ref)):
            rows = slice(i * OWN, (i + 1) * OWN)
            buf[n, rows, :HD] = ref[:, n * HD : (n + 1) * HD]
            buf[n, rows, HD:] = wide[i]
    x = lax.axis_index("x")
    for s in range(NX):
        outs[s][...] = buf[lax.rem(x + s, NX)]


def at(start, size):
    return pl.ds(pl.multiple_of(start, 32), size)


def split3(value):
    a = value.astype(BF16)
    r = value - a.astype(F32)
    b = r.astype(BF16)
    return a, b, (r - b.astype(F32)).astype(BF16)


def sort_keys(ids, tables, row, dyl, first, pieces, swapped, dst):
    for s in range(NX):
        for dc in range(2):
            ctx = ctx_of(ids, s, dyl, dc)
            near, far = (pieces, swapped)[dc]
            src, base = (near, 0) if s == 0 else (far, 2 * (s - 1) * OWN)
            for h in range(2):
                begin = base + first + h * BLK
                dst[at(tables[row, 2 * ctx + h] * BLK, BLK), :] = src[begin : begin + BLK, :]


def sort_rows(ids, tables, blocks, dst):
    for s in range(NX):
        ctx = ctx_of(ids, s, 0, 0)
        for h in range(2):
            dst[at(tables[1, 2 * ctx + h] * BLK, BLK), :] = blocks(s, h)


def sort_limits(ids, tables, limits):
    for s in range(NX):
        ctx = ctx_of(ids, s, 0, 0)
        for h in range(2):
            r = tables[1, 2 * ctx + h]
            limits[0, r] = tables[0, 2 * ctx + h]
            limits[1, r] = tables[2, 2 * ctx + h]
            limits[2, r] = tables[3, 2 * ctx + h]


def tile_limits(limits, i, dyl):
    b0, b1 = (QT * i) // BLK, (QT * i + QT - 1) // BLK
    row = lax.broadcasted_iota(jnp.int32, (1, QT), 1) + QT * i
    lim = jnp.zeros((1, QT), jnp.int32)
    for b in range(b0, b1 + 1):
        inside = jnp.logical_and(row >= b * BLK, row < (b + 1) * BLK)
        if dyl == 1:
            value = jnp.broadcast_to(limits[1, b] * BLK - 1, (1, QT))
        else:
            value = limits[dyl, b] * BLK + (row - b * BLK)
        lim = jnp.where(inside, value, lim)
    return lim, limits[dyl, b1] * BLK + (0 if dyl == 1 else BLK)


def list_work(limits, dyl, size, per, work, lims):
    count = jnp.int32(0)
    for i in range(NQT):
        lim, last = tile_limits(limits, i, dyl)
        lims[i] = lim
        n = lax.div(last + size - 1, size)

        def put(k, carry, i=i, count=count):
            work[0, count + k] = i
            work[1, count + k] = k
            return carry

        lax.fori_loop(0, n, put, 0)
        count = count + n
    lims[NQT] = jnp.full((1, QT), -1, jnp.int32)
    for u in range(per - 1):
        work[0, count + u] = NQT
        work[1, count + u] = 0
    return lax.div(count + per - 1, per)


def stats_kernel(tables, slope, *rest):
    ids = here()
    qo, kv, kv_c, kv_y, kv_yc = rest[0:4], rest[4:6], rest[6:8], rest[8:10], rest[10:12]
    qs, qt = rest[12:14]
    keys, limits, work, lims, tops, totals = rest[14:20]
    sort_keys(ids, tables, 3, 0, 0, kv, kv_c, keys)
    sort_keys(ids, tables, 3, 1, 0, kv_y, kv_yc, keys)
    sort_rows(ids, tables, lambda s, h: qo[s][h * BLK : (h + 1) * BLK, :], qs)
    qs[QROWS:, :] = jnp.zeros((QT, W), BF16)
    sort_limits(ids, tables, limits)
    m1, m2, m3 = split3(jnp.full((1, QT), slope[0] / SCALE, F32))
    for i in range(NQT):
        qt[i] = qs[i * QT : (i + 1) * QT, :].T
        qt[i, HD : HD + 16, :] = jnp.concatenate(
            [m1, m2, m3, m1, m2, m3, jnp.zeros((10, QT), BF16)], axis=0
        )
    qt[NQT] = jnp.zeros((W, QT), BF16)
    steps = list_work(limits, 2, SKC, SPER, work, lims)
    tops[...] = jnp.full(tops.shape, NEG, F32)
    totals[...] = jnp.zeros(totals.shape, F32)

    def step(j, carry):
        for u in range(SPER):
            item = j * SPER + u
            tile, chunk = work[0, item], work[1, item]
            s = jnp.dot(keys[at(chunk * SKC, SKC), :], qt[tile], preferred_element_type=F32)
            index = lax.broadcasted_iota(jnp.int32, (SKC, QT), 0)
            s = jnp.where(index <= lims[tile] - chunk * SKC, s, NEG)
            s = s.reshape(SKC // 8, 8, QT)
            top = jnp.max(s, axis=0)
            tops[tile, chunk] = top
            totals[tile, chunk] = jnp.sum(jnp.exp2((s - top[None]) * CEXP), axis=0)
        return carry

    lax.fori_loop(0, steps, step, 0)
    for i in range(NQT):
        top = jnp.max(jnp.max(tops[i], axis=0), axis=0, keepdims=True)
        total8 = jnp.sum(totals[i] * jnp.exp2((tops[i] - top) * CEXP), axis=0)
        total = jnp.sum(total8, axis=0, keepdims=True)
        l1, l2, l3 = split3(-(top + jnp.log(total) * (1.0 / SCALE)))
        qt[i, HD : HD + 16, :] = jnp.concatenate(
            [m1, m2, m3, m1, m2, m3, l1, l2, l3, jnp.zeros((7, QT), BF16)], axis=0
        )


def grads_loop(dyl, keys, vals, qs, qt, dos, dot, limits, dkey, dval, dq, work, lims):
    dkey[...] = jnp.zeros((HALF, W), F32)
    dval[...] = jnp.zeros((HALF, W), F32)
    steps = list_work(limits, dyl, GKC, GPER, work, lims)

    def step(j, carry):
        items = []
        for u in range(GPER):
            item = j * GPER + u
            tile, chunk = work[0, item], work[1, item]
            rows = at(chunk * GKC, GKC)
            cols = at(tile * QT, QT)
            kc = keys[rows, :]
            s = jnp.dot(kc, qt[tile], preferred_element_type=F32)
            dp = jnp.dot(vals[rows, :], dot[tile], preferred_element_type=F32)
            items.append((tile, chunk, rows, cols, kc, s, dp))
        parts = []
        for tile, chunk, rows, cols, kc, s, dp in items:
            index = lax.broadcasted_iota(jnp.int32, (GKC, QT), 0)
            p = jnp.where(index <= lims[tile] - chunk * GKC, jnp.exp2(s * CEXP), 0.0)
            ds = (p * dp).astype(BF16)
            dv = jnp.dot(p.astype(BF16), dos[cols, :], preferred_element_type=F32)
            dk = jnp.dot(ds, qs[cols, :], preferred_element_type=F32)
            d = lax.dot_general(ds, kc, (((0,), (0,)), ((), ())), preferred_element_type=F32)
            parts.append((rows, cols, dv, dk, d))
        for rows, cols, dv, dk, d in parts:
            dval[rows, :] += dv
            dkey[rows, :] += dk
            dq[cols, :] += d
        return carry

    lax.fori_loop(0, steps, step, 0)


def unsort(ids, tables, dyl, dc, dkey, dval, out):
    for s in range(NX):
        ctx = ctx_of(ids, s, dyl, dc)
        for h in range(2):
            rows = at(tables[0, 2 * ctx + h] * BLK, BLK)
            base = s * 2 * OWN + h * BLK
            out[base : base + BLK, :] = (dkey[rows, :] * SCALE).astype(BF16)
            out[base + OWN : base + OWN + BLK, :] = dval[rows, :].astype(BF16)


def grads_other_kernel(tables, *rest):
    ids = here()
    qo, kv_y, kv_yc = rest[0:4], rest[4:6], rest[6:8]
    dor, qs, qt = rest[8:11]
    dos, dot, dq, keep, send = rest[11:16]
    keys, vals, dkey, dval, work, lims, flat, outs, limits = rest[16:25]
    sort_keys(ids, tables, 0, 1, 0, kv_y, kv_yc, keys)
    sort_keys(ids, tables, 0, 1, OWN, kv_y, kv_yc, vals)
    sort_limits(ids, tables, limits)
    for n in range(64):
        flat[n * 20 : (n + 1) * 20, :] = dor[n]

    def block(s, h):
        x = lax.rem(ids[0] + (NX - s), NX)
        return flat[at(x * OWN + h * BLK, BLK), :]

    sort_rows(ids, tables, block, dos)
    sort_rows(ids, tables, lambda s, h: qo[s][OWN + h * BLK : OWN + (h + 1) * BLK, :], outs)
    for i in range(NQT):
        cols = slice(i * QT, (i + 1) * QT)
        prod = dos[cols, :].astype(F32) * outs[cols, :].astype(F32)
        delta = jnp.sum(prod.T, axis=0, keepdims=True)
        d1, d2, d3 = split3(-delta)
        dot[i] = dos[cols, :].T
        dot[i, HD : HD + 16, :] = jnp.concatenate(
            [d1, d2, d3, jnp.zeros((13, QT), BF16)], axis=0
        )
    dot[NQT] = jnp.zeros((W, QT), BF16)
    dos[QROWS:, :] = jnp.zeros((QT, W), BF16)
    dq[...] = jnp.zeros((DROWS, W), F32)
    grads_loop(1, keys, vals, qs, qt, dos, dot, limits, dkey, dval, dq, work, lims)
    unsort(ids, tables, 1, 0, dkey, dval, keep)
    unsort(ids, tables, 1, 1, dkey, dval, send)


def grads_own_kernel(tables, *rest):
    ids = here()
    kv, kv_c = rest[0:2], rest[2:4]
    qs, qt, dos, dot, dq_in = rest[4:9]
    dqo, keep, send = rest[9:13], rest[13], rest[14]
    keys, vals, dkey, dval, work, lims, dq, limits = rest[15:23]
    sort_keys(ids, tables, 0, 0, 0, kv, kv_c, keys)
    sort_keys(ids, tables, 0, 0, OWN, kv, kv_c, vals)
    sort_limits(ids, tables, limits)
    dq[...] = dq_in[...]
    grads_loop(0, keys, vals, qs, qt, dos, dot, limits, dkey, dval, dq, work, lims)
    unsort(ids, tables, 0, 0, dkey, dval, keep)
    unsort(ids, tables, 0, 1, dkey, dval, send)
    for s in range(NX):
        ctx = ctx_of(ids, s, 0, 0)
        for h in range(2):
            rows = at(tables[1, 2 * ctx + h] * BLK, BLK)
            dqo[s][h * BLK : (h + 1) * BLK, :] = (dq[rows, :] * SCALE).astype(BF16)


def fold(total, out):
    rows = total.shape[0] // 8
    out[...] = total[: 7 * rows, :]
    for i in range(7):
        out[i * rows : (i + 1) * rows, HD:] = total[7 * rows :, i * 16 : (i + 1) * 16]


def unfold(folded, out):
    rows = folded.shape[0] // 7
    out[: 7 * rows, :] = folded[...]
    for i in range(7):
        out[7 * rows :, i * 16 : (i + 1) * 16] = folded[i * rows : (i + 1) * rows, HD:]


def add_kernel(a, b, out):
    fold((a[...].astype(F32) + b[...].astype(F32)).astype(BF16), out)


def add_own_kernel(a, b, folded, *rest):
    outs, c = rest[0:4], rest[4]
    c[:, HD:] = jnp.zeros((NX * 2 * OWN, W - HD), BF16)
    unfold(folded, c)
    for s in range(NX):
        rows = slice(s * 2 * OWN, (s + 1) * 2 * OWN)
        total = a[rows, :].astype(F32) + b[rows, :].astype(F32) + c[rows, :].astype(F32)
        fold(total.astype(BF16), outs[s])


def unpack_kernel(*rest):
    dqs, dkvs, outs, buf = rest[0:4], rest[4:8], rest[8:11], rest[11]
    x = lax.axis_index("x")
    for s in range(NX):
        head = lax.rem(x + s, NX)
        buf[head, :OWN, :] = dqs[s][...]
        unfold(dkvs[s], buf.at[head, OWN:, :])
    for n in range(NX):
        for i in range(3):
            outs[i][:, n * HD : (n + 1) * HD] = buf[n, i * OWN : (i + 1) * OWN, :HD]


def shift(value, by, flip=False):
    pairs = []
    for x in range(NX):
        for yl in range(2):
            pairs.append((2 * x + yl, 2 * ((x + by) % NX) + (1 - yl if flip else yl)))
    return lax.ppermute(value, ("x", "yl"), pairs)


def swap_core(value):
    return lax.ppermute(value, "c", [(0, 1), (1, 0)])


def worklist(size, keys, per):
    items = NQT * (keys // size) + per
    return [pltpu.SMEM((2, items), jnp.int32), pltpu.VMEM((NQT + 1, 1, QT), jnp.int32)]


def plan_tables(plan):
    block = jnp.arange(32, dtype=jnp.int32)
    half = (block >> 2) & 1
    group = (block >> 1) & 3
    before = plan[None, :] < plan[:, None]
    same_half = half[None, :] == half[:, None]
    same_group = group[None, :] == group[:, None]

    def count(m):
        return jnp.sum(jnp.where(jnp.logical_and(before, m), 1, 0), axis=1, dtype=jnp.int32)

    return jnp.stack([count(same_half), count(same_group), count(jnp.logical_not(same_half)), plan])


def on_device(queries, keys, values, out_fwd, d_out, plan):
    piece = ((2 * OWN, W), BF16)
    stack = ((NX * 2 * OWN, W), BF16)
    x = lax.axis_index("x")
    tables = plan_tables(plan)
    head_id = (lax.axis_index("yh") * 8 + lax.axis_index("z")) * NX + x
    slope = jnp.exp2(-8.0 * (head_id + 1).astype(F32) / 64.0).reshape(1)

    buf = [pltpu.VMEM((NX, 2 * OWN, W), BF16)]
    kv = call(functools.partial(pack_kernel, "kv"), [piece] * 4, buf, "pack_kv")(plan, keys, values)
    kv, d_out = lax.optimization_barrier((kv, d_out))
    (d_pack,) = call(cotangent_pack_kernel, [((64, 20, W), BF16)], [], "cotangent_pack")(d_out)
    d_rows = lax.all_to_all(d_pack, ("x", "yh", "z"), 0, 0)
    kv = [kv[0], jnp.concatenate([shift(kv[s], s) for s in (1, 2, 3)])]
    kv_y = [shift(a, 0, True) for a in kv]
    kv_c = [swap_core(a) for a in kv]
    qo = call(functools.partial(pack_kernel, "qo"), [piece] * 4, buf, "pack_qo", 2)(
        plan, queries, out_fwd, kv[1], tables
    )
    qo = [qo[0]] + [shift(qo[s], s) for s in (1, 2, 3)]
    kv_y, qo, d_rows = lax.optimization_barrier((kv_y, qo, d_rows))
    kv_yc = [swap_core(a) for a in kv_y]

    limits = pltpu.SMEM((3, 8), jnp.int32)
    qs, qt = call(
        stats_kernel,
        [((DROWS, W), BF16), ((NQT + 1, W, QT), BF16)],
        [pltpu.VMEM((2 * HALF, W), BF16), limits]
        + worklist(SKC, 2 * HALF, SPER)
        + [pltpu.VMEM((NQT + 1, 2 * HALF // SKC, 8, QT), F32)] * 2,
        "stats",
    )(tables, slope, *qo, *kv, *kv_c, *kv_y, *kv_yc)
    accs = [pltpu.VMEM((HALF, W), BF16)] * 2 + [pltpu.VMEM((HALF, W), F32)] * 2
    accs = accs + worklist(GKC, HALF, GPER)
    dos, dot, dq, keep, send = call(
        grads_other_kernel,
        [((DROWS, W), BF16), ((NQT + 1, W, QT), BF16), ((DROWS, W), F32), stack, stack],
        accs + [pltpu.VMEM((QROWS, W), BF16)] * 2 + [limits],
        "grads_other",
    )(tables, *qo, *kv_y, *kv_yc, d_rows, qs, qt)
    (dkv_y,) = call(add_kernel, [((NX * 2 * OWN // 8 * 7, W), BF16)], [], "add_other")(keep, swap_core(send))
    dq, dkv_y = lax.optimization_barrier((dq, dkv_y))
    dkv_y = shift(dkv_y, 0, True)

    *dqs, keep, send = call(
        grads_own_kernel,
        [((OWN, W), BF16)] * 4 + [stack, stack],
        accs + [pltpu.VMEM((DROWS, W), F32), limits],
        "grads_own",
    )(tables, *kv, *kv_c, qs, qt, dos, dot, dq)
    dqs[1], dqs[2], dkv_y = lax.optimization_barrier((dqs[1], dqs[2], dkv_y))
    swapped = swap_core(send)
    dqs = [dqs[0]] + [shift(dqs[s], -s) for s in (1, 2, 3)]
    dkvs = call(
        add_own_kernel,
        [((2 * OWN // 8 * 7, W), BF16)] * 4,
        [pltpu.VMEM((NX * 2 * OWN, W), BF16)],
        "add_own",
    )(keep, swapped, dkv_y)
    dkvs = [dkvs[0]] + [shift(dkvs[s], -s) for s in (1, 2, 3)]
    return tuple(
        call(
            unpack_kernel,
            [((OWN, NX * HD), BF16)] * 3,
            [pltpu.VMEM((NX, 3 * OWN, W), BF16)],
            "unpack",
        )(*dqs, *dkvs)
    )


def solution(mesh):
    devices = mesh.devices.reshape(4, 2, 2, 2, 8)
    fine = Mesh(devices, ("x", "yl", "c", "yh", "z"))
    ctx, head = ("x", "yl", "c"), ("yh", "z")
    tile = P(ctx, head)
    return jax.shard_map(
        on_device,
        mesh=fine,
        in_specs=(tile, tile, tile, tile, P(ctx + head, None), P()),
        out_specs=(tile, tile, tile),
        check_vma=False,
    )
```
